512 devices in a mesh: dp: 2 (over core), seq: 16 (over y, x), head: 16 (over z).
Axes of the slice: x: 4, y: 4, z: 16, core: 2. Of those that a mesh axis runs over, the one named last changes fastest.
Arguments:
- queries: bfloat16 [65536, 32, 128], P(('dp', 'seq', 'head')), parts along dimension 0, may hold values from -6 to 6
- keys: bfloat16 [65536, 4, 128], P(('dp', 'seq', 'head')), parts along dimension 0, may hold values from -6 to 6
- values: bfloat16 [65536, 4, 128], P(('dp', 'seq', 'head')), parts along dimension 0, may hold values from -6 to 6
- out_grad: bfloat16 [65536, 32, 128], P(('dp', 'seq', 'head')), parts along dimension 0, may hold values from -24 to 24
- kept_blocks: int32 [4, 256, 1], replicated, may hold values from 0 to 255, as said below
- sink_blocks: int32 [4], replicated, may hold values from 1 to 3
- window_blocks: int32 [4], replicated, may hold values from 2 to 4
Outputs:
- grad_queries: bfloat16 [65536, 32, 128], P(('dp', 'seq', 'head')), parts along dimension 0
- grad_keys: bfloat16 [65536, 4, 128], P(('dp', 'seq', 'head')), parts along dimension 0
- grad_values: bfloat16 [65536, 4, 128], P(('dp', 'seq', 'head')), parts along dimension 0
The draws below stay inside these ranges and needn't reach their ends.
There are 2 independent parts, one for each index of `dp`. The reference program is written for one: setup_inputs(seed, part) draws one part's arguments, and reference() takes and returns one part's arrays. A program takes and returns all parts, laid end to end along the dimension named above; an argument that names none is the same for every part. Nothing has to cross between parts.
Inputs may be any that keep to these rules, and one draw needn't show every extreme that they name: `kept_blocks`: entries that name a block after the query block are ignored; entries may name sink or window blocks. For each key head and each index of seq, the 16 entries of that index's query blocks name blocks held by one index of seq at most 2 times in all, and exactly 2 times for some index of seq.
All inputs are finite; a program needn't handle non-finite values.
Results may differ from the reference program's by a relative error of at most 0.0076.
Values may be sent and summed in bfloat16 or wider, within the bound.
A program may use at most 128 MiB of HBM per device.

```python
import math
import jax
import jax.numpy as jnp
from jax import lax

QHEADS = 32
KVH = 4
HD = 128
BLK = 128
KEEP = 1
SINK_MOST = 3
WIN_MOST = 4
SEQ_DEV = 2048
TOKENS = 32768
BLOCKS = 256
CAP = 2


def draw_keys(key, part):
    base = jnp.clip(jax.random.normal(jax.random.fold_in(key, 1), (TOKENS, KVH, HD), jnp.float32), -6.0, 6.0)
    return base.astype(jnp.bfloat16)


def draw_queries(key, part):
    base = jnp.clip(jax.random.normal(jax.random.fold_in(key, 2), (TOKENS, QHEADS, HD), jnp.float32), -6.0, 6.0)
    return base.astype(jnp.bfloat16)


def draw_kept_blocks(key, part):
    per_index = SEQ_DEV // BLK
    seq_count = BLOCKS // per_index
    entries = per_index * KEEP
    places = seq_count * CAP
    owner_of_place = jnp.arange(places, dtype=jnp.int32) // CAP

    def one_list(subkey):
        favored = jax.random.randint(jax.random.fold_in(subkey, 1), (), 0, seq_count)
        ranking = jax.random.permutation(jax.random.fold_in(subkey, 2), places).astype(jnp.int32)
        ranking = ranking - jnp.where(owner_of_place == favored, places, 0)
        picked = owner_of_place[jnp.argsort(ranking)][:entries]
        picked = picked[jax.random.permutation(jax.random.fold_in(subkey, 3), entries)]
        inner = jax.random.randint(jax.random.fold_in(subkey, 4), (entries,), 0, per_index)
        return (picked * per_index + inner).reshape(per_index, KEEP)
    subkeys = jax.vmap(lambda index: jax.random.fold_in(key, 1000 + index))(jnp.arange(KVH * seq_count))
    lists = jax.vmap(one_list)(subkeys)
    return lists.reshape(KVH, BLOCKS, KEEP).astype(jnp.int32)


def set_ends(values, rng, smallest, largest):
    longest = values.shape.index(max(values.shape))
    spots = []
    for shift in (0, 1):
        where = [jax.random.randint(jax.random.fold_in(rng, axis), (), 0, length) for axis, length in enumerate(values.shape)]
        where[longest] = (where[longest] + shift) % values.shape[longest]
        spots.append(tuple(where))
    return values.at[spots[0]].set(smallest).at[spots[1]].set(largest)


def steps_of(rng, dims, shards, low, high):
    gain, own = 1.0, jax.random.fold_in(rng, 6)
    for position, shards_of in shards:
        heights = jnp.exp(jax.random.uniform(jax.random.fold_in(own, position), (shards_of,), jnp.float32, low / len(shards), high / len(shards)))
        gain = gain * jnp.repeat(heights, dims[position] // shards_of).reshape([-1 if axis == position else 1 for axis in range(len(dims))])
    return gain


def normal_values(key, shape, deviation, most, pieces=(), kind=jnp.bfloat16):
    values = deviation * jax.random.normal(key, shape, jnp.float32)
    if pieces:
        values = values * steps_of(key, shape, pieces, -0.22, 0.18)
    return jnp.clip(values, -most, most).astype(kind)


def setup_inputs(seed: int = 0, part: int = 0) -> dict:
    streams_of = jax.random.split(jax.random.key(seed), 8)
    part_keys = jax.random.split(jax.random.fold_in(streams_of[7], part), 8)
    queries = draw_queries(jax.random.fold_in(jax.random.fold_in(streams_of[7], part), 71), part)
    keys = draw_keys(jax.random.fold_in(jax.random.fold_in(streams_of[7], part), 71), part)
    values = normal_values(part_keys[2], (TOKENS, KVH, HD), 1.0, 6.0, ((0, 256),))
    out_grad = normal_values(part_keys[3], (TOKENS, QHEADS, HD), 4.0, 24.0, ((0, 256),))
    kept_blocks = draw_kept_blocks(jax.random.fold_in(streams_of[7], 71), part)
    sink_blocks = set_ends(jax.random.randint(streams_of[5], (KVH,), 1, SINK_MOST + 1), jax.random.fold_in(streams_of[5], 1), 1, SINK_MOST).astype(jnp.int32)
    window_blocks = set_ends(jax.random.randint(streams_of[6], (KVH,), 2, WIN_MOST + 1), jax.random.fold_in(streams_of[6], 1), 2, WIN_MOST).astype(jnp.int32)
    return dict(queries=queries, keys=keys, values=values, out_grad=out_grad, kept_blocks=kept_blocks, sink_blocks=sink_blocks, window_blocks=window_blocks)


def slot_table(query_blocks, kept_rows, sink_count, window_count):
    current = query_blocks[:, None]
    number = query_blocks.shape[0]
    sink_ids = jnp.broadcast_to(jnp.arange(SINK_MOST, dtype=jnp.int32)[None, :], (number, SINK_MOST))
    sink_ok = (sink_ids < sink_count) & (sink_ids <= current) & (current - sink_ids >= window_count)
    offsets = jnp.arange(WIN_MOST, dtype=jnp.int32)[None, :]
    window_ids = current - offsets
    window_ok = (offsets < window_count) & (window_ids >= 0)
    kept_ok = (kept_rows <= current) & (kept_rows >= sink_count) & (current - kept_rows >= window_count)
    fresh = []
    for entry in range(kept_rows.shape[1]):
        repeated = jnp.zeros((number,), dtype=bool)
        for earlier in range(entry):
            repeated = repeated | (kept_rows[:, earlier] == kept_rows[:, entry])
        fresh.append(jnp.logical_not(repeated))
    kept_ok = kept_ok & jnp.stack(fresh, axis=1)
    slot_ids = jnp.concatenate([sink_ids, window_ids, kept_rows], axis=1)
    slot_ok = jnp.concatenate([sink_ok, window_ok, kept_ok], axis=1)
    return (jnp.maximum(slot_ids, 0).astype(jnp.int32), slot_ok)

def slot_mask(slot_ok):
    number, slots = slot_ok.shape
    within = jnp.arange(BLK, dtype=jnp.int32)
    diagonal = within[None, :] <= within[:, None]
    on_diagonal = jnp.arange(slots, dtype=jnp.int32) == SINK_MOST
    allowed = slot_ok[:, None, :, None] & (jnp.logical_not(on_diagonal)[None, None, :, None] | diagonal[None, :, None, :])
    return allowed.reshape(number, BLK, slots * BLK)

def reference(queries, keys, values, out_grad, kept_blocks, sink_blocks, window_blocks):
    tokens = queries.shape[0]
    count = tokens // BLK
    group = QHEADS // KVH
    scale = 1.0 / math.sqrt(HD)
    slots = SINK_MOST + WIN_MOST + KEEP
    all_blocks = jnp.arange(count, dtype=jnp.int32)

    def per_group(kv_head):
        kept_rows = lax.dynamic_index_in_dim(kept_blocks, kv_head, 0, keepdims=False)
        sink_count = lax.dynamic_index_in_dim(sink_blocks, kv_head, 0, keepdims=False)
        window_count = lax.dynamic_index_in_dim(window_blocks, kv_head, 0, keepdims=False)
        slot_ids, slot_ok = slot_table(all_blocks, kept_rows, sink_count, window_count)
        allowed = slot_mask(slot_ok)
        key_blocks = lax.dynamic_index_in_dim(keys, kv_head, 1, keepdims=False).reshape(count, BLK, HD)
        value_blocks = lax.dynamic_index_in_dim(values, kv_head, 1, keepdims=False).reshape(count, BLK, HD)
        slot_keys = key_blocks[slot_ids].reshape(count, slots * BLK, HD).astype(jnp.float32)
        slot_values = value_blocks[slot_ids].reshape(count, slots * BLK, HD).astype(jnp.float32)

        def per_head(carry, member):
            head = kv_head * group + member
            query_rows = lax.dynamic_index_in_dim(queries, head, 1, keepdims=False).reshape(count, BLK, HD).astype(jnp.float32)
            grad_rows = lax.dynamic_index_in_dim(out_grad, head, 1, keepdims=False).reshape(count, BLK, HD).astype(jnp.float32)
            scores = jnp.einsum('ntd,nud->ntu', query_rows, slot_keys) * scale
            scores = jnp.where(allowed, scores, -jnp.inf)
            top = lax.optimization_barrier(jnp.max(scores, axis=2, keepdims=True))
            lse = top + jnp.log(lax.optimization_barrier(jnp.sum(jnp.exp(scores - top), axis=2, keepdims=True)))
            probs = jnp.exp(scores - lse)
            probs_low = probs.astype(jnp.bfloat16)
            dprobs = jnp.einsum('ntd,nud->ntu', grad_rows, slot_values)
            delta = lax.optimization_barrier(jnp.sum(probs * dprobs, axis=2, keepdims=True))
            dscores = (probs * (dprobs - delta)).astype(jnp.bfloat16)
            dscores_wide = dscores.astype(jnp.float32)
            grad_q = (jnp.einsum('ntu,nud->ntd', dscores_wide, slot_keys) * scale).astype(jnp.bfloat16)
            key_terms = jnp.einsum('ntu,ntd->nud', dscores_wide, query_rows) * scale
            value_terms = jnp.einsum('ntu,ntd->nud', probs_low.astype(jnp.float32), grad_rows)
            key_sum = carry[0].at[slot_ids].add(key_terms.reshape(count, slots, BLK, HD))
            value_sum = carry[1].at[slot_ids].add(value_terms.reshape(count, slots, BLK, HD))
            return ((key_sum, value_sum), grad_q.reshape(tokens, HD))
        start = (jnp.zeros((count, BLK, HD), jnp.float32), jnp.zeros((count, BLK, HD), jnp.float32))
        (key_sum, value_sum), grad_q = lax.scan(per_head, start, jnp.arange(group, dtype=jnp.int32))
        return (grad_q, key_sum.reshape(tokens, HD), value_sum.reshape(tokens, HD))
    grad_q, grad_k, grad_v = lax.map(per_group, jnp.arange(KVH, dtype=jnp.int32))
    grad_queries = jnp.transpose(grad_q.reshape(QHEADS, tokens, HD), (1, 0, 2))
    grad_keys = jnp.transpose(grad_k, (1, 0, 2)).astype(jnp.bfloat16)
    grad_values = jnp.transpose(grad_v, (1, 0, 2)).astype(jnp.bfloat16)
    return (grad_queries, grad_keys, grad_values)
```

```python
import math

import jax
import jax.numpy as jnp
from jax import lax
from jax.experimental import pallas as pl
from jax.experimental.pallas import tpu as pltpu
from jax.sharding import PartitionSpec as P

BLK = 128
SINK_MOST = 3
WIN_MOST = 4
SLOTS = 8
N = 16
KVH = 4
GROUP = 8
HD = 128
CAP = 2
ROWS = 32
PIECE = (2, ROWS, HD)
MESH = pl.DeviceIdType.MESH
VMEM_LIMIT = 48 * 1024 * 1024


def remote(src, dst, send, recv, device):
    return pltpu.make_async_remote_copy(
        src_ref=src, dst_ref=dst, send_sem=send, recv_sem=recv, device_id=device, device_id_type=MESH
    )


def neighbours(seq, head):
    wrap_up = (head == N - 1).astype(jnp.int32)
    wrap_down = (head == 0).astype(jnp.int32)
    after = {"seq": lax.rem(seq + wrap_up, N), "head": lax.rem(head + 1, N)}
    before = {"seq": lax.rem(seq + N - wrap_down, N), "head": lax.rem(head + N - 1, N)}
    return before, after


def greet(seq, head, before, after):
    barrier = pltpu.get_barrier_semaphore()
    for k in range(1, N):
        pl.semaphore_signal(
            barrier, inc=1, device_id={"head": lax.rem(head + k, N)}, device_id_type=MESH
        )
        pl.semaphore_signal(
            barrier, inc=1, device_id={"seq": lax.rem(seq + k, N)}, device_id_type=MESH
        )
    pl.semaphore_signal(barrier, inc=1, device_id=before, device_id_type=MESH)
    pl.semaphore_signal(barrier, inc=1, device_id=after, device_id_type=MESH)
    pl.semaphore_wait(barrier, 2 * (N - 1) + 2)


def fetch_kernel(
    table, own, sink, win, kept,
    rows_in, slots_out, slots_in, far_out, piece, pieces,
    sw, rw, s1, r1, s2, r2, s3, r3, ss1, rs1, ss2, rs2, ss3, rs3,
):
    seq, head = lax.axis_index("seq"), lax.axis_index("head")
    before, after = neighbours(seq, head)
    greet(seq, head, before, after)

    steps = [remote(own, win.at[0], sw.at[0], rw.at[0], after)]
    for w in range(1, WIN_MOST - 1):
        steps.append(remote(win.at[w - 1], win.at[w], sw.at[w], rw.at[w], after))
    steps[0].start()

    def sink_send(k):
        return remote(own.at[k], piece, ss1.at[k], rs1.at[0], {"seq": k})

    @pl.when((seq == 0) & (head < SINK_MOST))
    def _():
        for k in range(1, N):
            sink_send(k).start()

    first = []
    for k in range(1, N):
        to = lax.rem(head + k, N)
        first.append(remote(own.at[to], rows_in.at[head], s1.at[k], r1.at[k], {"head": to}))
        first[-1].start()
    rows_in[head] = own[head]

    def piece_send(k):
        return remote(piece, pieces.at[head], ss2.at[k], rs2.at[head], {"head": lax.rem(head + k, N)})

    @pl.when((seq == 0) & (head < SINK_MOST))
    def _():
        piece[...] = own[0]

    @pl.when((seq > 0) & (head < SINK_MOST))
    def _():
        remote(own.at[0], piece, ss1.at[0], rs1.at[0], {"seq": 0}).wait_recv()

    @pl.when(head < SINK_MOST)
    def _():
        for k in range(1, N):
            piece_send(k).start()
        pieces[head] = piece[...]

    steps[0].wait_recv()
    steps[1].start()

    for copy in first:
        copy.wait_recv()
    for k in range(N):
        for c in range(CAP):
            slots_out[k, c] = rows_in[table[0, k * CAP + c]]
    second = []
    for k in range(1, N):
        to = lax.rem(seq + k, N)
        second.append(remote(slots_out.at[to], slots_in.at[seq], s2.at[k], r2.at[k], {"seq": to}))
        second[-1].start()
    slots_in[seq] = slots_out[seq]

    for b in range(SINK_MOST):

        @pl.when(head != b)
        def _():
            remote(piece, pieces.at[b], ss2.at[0], rs2.at[b], {"head": b}).wait_recv()

    spread = []
    for k in range(1, N):
        to = lax.rem(seq + k, N)
        spread.append(remote(pieces, sink.at[seq], ss3.at[k], rs3.at[k], {"seq": to}))
        spread[-1].start()
    sink[seq] = pieces[...]

    steps[1].wait_recv()
    steps[2].start()

    for copy in second:
        copy.wait_recv()
    for k in range(N):
        far_out[k] = slots_in[table[1, k], table[1, N + k]]
    third = []
    for k in range(1, N):
        to = lax.rem(head + k, N)
        third.append(remote(far_out.at[to], kept.at[head], s3.at[k], r3.at[k], {"head": to}))
        third[-1].start()
    kept[head] = far_out[head]

    steps[2].wait_recv()
    for copy in spread:
        copy.wait_recv()
    for copy in third:
        copy.wait_recv()
    for copy in steps + first + second + spread + third:
        copy.wait_send()

    @pl.when((seq == 0) & (head < SINK_MOST))
    def _():
        for k in range(1, N):
            sink_send(k).wait_send()

    @pl.when(head < SINK_MOST)
    def _():
        for k in range(1, N):
            piece_send(k).wait_send()


def fetch(table, own):
    sems = []
    for count in (3, N, N, N):
        sems += [pltpu.SemaphoreType.DMA((count,)), pltpu.SemaphoreType.DMA((count,))]
    sems += [pltpu.SemaphoreType.DMA((N,)), pltpu.SemaphoreType.DMA((1,))]
    sems += [pltpu.SemaphoreType.DMA((N,)), pltpu.SemaphoreType.DMA((N,))]
    sems += [pltpu.SemaphoreType.DMA((N,)), pltpu.SemaphoreType.DMA((N,))]
    vmem = pl.BlockSpec(memory_space=pltpu.VMEM)
    return pl.pallas_call(
        fetch_kernel,
        out_shape=(
            jax.ShapeDtypeStruct((N, SINK_MOST) + PIECE, jnp.bfloat16),
            jax.ShapeDtypeStruct((WIN_MOST - 1, N) + PIECE, jnp.bfloat16),
            jax.ShapeDtypeStruct((N,) + PIECE, jnp.bfloat16),
        ),
        in_specs=[pl.BlockSpec(memory_space=pltpu.SMEM), vmem],
        out_specs=(vmem, vmem, vmem),
        scratch_shapes=[
            pltpu.VMEM((N,) + PIECE, jnp.bfloat16),
            pltpu.VMEM((N, CAP) + PIECE, jnp.bfloat16),
            pltpu.VMEM((N, CAP) + PIECE, jnp.bfloat16),
            pltpu.VMEM((N,) + PIECE, jnp.bfloat16),
            pltpu.VMEM(PIECE, jnp.bfloat16),
            pltpu.VMEM((SINK_MOST,) + PIECE, jnp.bfloat16),
        ]
        + sems,
        compiler_params=pltpu.CompilerParams(
            collective_id=0, has_side_effects=True, vmem_limit_bytes=VMEM_LIMIT
        ),
        name="fetch",
    )(table, own)


def give_kernel(
    table, tsink, tkept, near, out,
    rows, slots_out, slots_in, run, back, back_in,
    sink_in, pieces, pieces_in, piece, whole, hop_out, hop_in, total,
    sw, rw, s1, r1, s2, r2, s3, r3, ss1, rs1, ss2, rs2, ss3, rs3,
):
    seq, head = lax.axis_index("seq"), lax.axis_index("head")
    before, after = neighbours(seq, head)
    greet(seq, head, before, after)
    low, wide = jnp.bfloat16, jnp.float32

    first = []
    for k in range(1, N):
        to = lax.rem(head + k, N)
        first.append(remote(tkept.at[to], rows.at[head], s1.at[k], r1.at[k], {"head": to}))
        first[-1].start()

    hop_out[0] = near[WIN_MOST - 1].astype(low)
    hops = [
        remote(hop_out.at[w], hop_in.at[w], sw.at[w], rw.at[w], before) for w in range(WIN_MOST - 1)
    ]
    hops[0].start()

    spread = []
    for k in range(1, N):
        to = lax.rem(seq + k, N)
        spread.append(remote(tsink.at[to], sink_in.at[seq], ss3.at[k], rs3.at[k], {"seq": to}))
        spread[-1].start()

    sink_in[seq] = tsink[seq]
    rows[head] = tkept[head]
    rows[N] = jnp.zeros(PIECE, low)

    for copy in first:
        copy.wait_recv()
    for k in range(N):
        for c in range(CAP):
            slots_out[k, c] = rows[table[2, k * CAP + c]]
    second = []
    for k in range(1, N):
        to = lax.rem(seq + k, N)
        second.append(remote(slots_out.at[to], slots_in.at[seq], s2.at[k], r2.at[k], {"seq": to}))
        second[-1].start()
    slots_in[seq] = slots_out[seq]

    hops[0].wait_recv()
    hop_out[1] = (near[2] + hop_in[0].astype(wide)).astype(low)
    hops[1].start()

    for copy in spread:
        copy.wait_recv()
    for b in range(SINK_MOST):
        term = sink_in[0, b].astype(wide)
        for k in range(1, N):
            term = term + sink_in[k, b].astype(wide)
        pieces[b] = term.astype(low)

    def piece_send(b):
        return remote(pieces.at[b], pieces_in.at[head], ss2.at[b], rs2.at[head], {"head": b})

    for b in range(SINK_MOST):

        @pl.when(head != b)
        def _():
            piece_send(b).start()

    run[...] = jnp.zeros(run.shape, wide)
    for copy in second:
        copy.wait_recv()
    for k in range(N):
        for c in range(CAP):
            i = k * CAP + c
            run[i] = slots_in[k, c].astype(wide) + run[table[3, i]]
    for k in range(N):
        back[k] = run[table[4, k]].astype(low)
    third = []
    for k in range(1, N):
        to = lax.rem(head + k, N)
        third.append(remote(back.at[to], back_in.at[head], s3.at[k], r3.at[k], {"head": to}))
        third[-1].start()
    back_in[head] = back[head]

    hops[1].wait_recv()
    hop_out[2] = (near[1] + hop_in[1].astype(wide)).astype(low)
    hops[2].start()

    def whole_send():
        return remote(piece, whole.at[seq], ss1.at[0], rs1.at[seq], {"seq": 0})

    @pl.when(head < SINK_MOST)
    def _():
        pieces_in[head] = pieces[head]
        for k in range(1, N):
            frm = lax.rem(head + k, N)
            remote(pieces.at[0], pieces_in.at[frm], ss2.at[0], rs2.at[frm], {"head": frm}).wait_recv()
        term = pieces_in[0].astype(wide)
        for k in range(1, N):
            term = term + pieces_in[k].astype(wide)
        piece[...] = term.astype(low)

    @pl.when((head < SINK_MOST) & (seq > 0))
    def _():
        whole_send().start()

    hops[2].wait_recv()
    total[...] = near[0] + hop_in[2].astype(wide)
    for copy in third:
        copy.wait_recv()
    total[...] = total[...] + back_in[...].astype(wide)

    @pl.when((head < SINK_MOST) & (seq == 0))
    def _():
        whole[0] = piece[...]
        for k in range(1, N):
            remote(piece, whole.at[k], ss1.at[0], rs1.at[k], {"seq": k}).wait_recv()
        total[...] = total[...] + whole[...].astype(wide)

    out[...] = total[...].astype(low)

    for copy in hops + first + second + spread + third:
        copy.wait_send()
    for b in range(SINK_MOST):

        @pl.when(head != b)
        def _():
            piece_send(b).wait_send()

    @pl.when((head < SINK_MOST) & (seq > 0))
    def _():
        whole_send().wait_send()


def give(table, tsink, tkept, near):
    sems = []
    for count in (3, N, N, N):
        sems += [pltpu.SemaphoreType.DMA((count,)), pltpu.SemaphoreType.DMA((count,))]
    sems += [pltpu.SemaphoreType.DMA((1,)), pltpu.SemaphoreType.DMA((N,))]
    sems += [pltpu.SemaphoreType.DMA((SINK_MOST,)), pltpu.SemaphoreType.DMA((N,))]
    sems += [pltpu.SemaphoreType.DMA((N,)), pltpu.SemaphoreType.DMA((N,))]
    vmem = pl.BlockSpec(memory_space=pltpu.VMEM)
    low, wide = jnp.bfloat16, jnp.float32
    return pl.pallas_call(
        give_kernel,
        out_shape=jax.ShapeDtypeStruct((N,) + PIECE, low),
        in_specs=[pl.BlockSpec(memory_space=pltpu.SMEM), vmem, vmem, vmem],
        out_specs=vmem,
        scratch_shapes=[
            pltpu.VMEM((N + 1,) + PIECE, low),
            pltpu.VMEM((N, CAP) + PIECE, low),
            pltpu.VMEM((N, CAP) + PIECE, low),
            pltpu.VMEM((N * CAP + 1,) + PIECE, wide),
            pltpu.VMEM((N,) + PIECE, low),
            pltpu.VMEM((N,) + PIECE, low),
            pltpu.VMEM((N, SINK_MOST) + PIECE, low),
            pltpu.VMEM((SINK_MOST,) + PIECE, low),
            pltpu.VMEM((N,) + PIECE, low),
            pltpu.VMEM(PIECE, low),
            pltpu.VMEM((N,) + PIECE, low),
            pltpu.VMEM((WIN_MOST - 1, N) + PIECE, low),
            pltpu.VMEM((WIN_MOST - 1, N) + PIECE, low),
            pltpu.VMEM((N,) + PIECE, wide),
        ]
        + sems,
        compiler_params=pltpu.CompilerParams(
            collective_id=1, has_side_effects=True, vmem_limit_bytes=VMEM_LIMIT
        ),
        name="give",
    )(table, tsink, tkept, near)


COLS = 256
PAIR = 2
NT = (((1,), (1,)), ((), ()))
NN = (((1,), (0,)), ((), ()))
TN = (((0,), (0,)), ((), ()))


def attend_kernel(
    bias, q, g, sink, own, win, kept, dq, tsink, tkept, near, kbuf, vbuf, qbuf, gbuf, pbuf, sbuf, dqbuf
):
    pair = pl.program_id(0)
    low, wide = jnp.bfloat16, jnp.float32
    scale = 1.0 / math.sqrt(HD)
    columns = BLK * GROUP

    for m in range(PAIR):
        rows = slice(m * GROUP, (m + 1) * GROUP)
        qbuf[...] = q[...].astype(wide)[:, rows].reshape(columns, HD).astype(low)
        gbuf[...] = g[...].astype(wide)[:, rows].reshape(columns, HD).astype(low)
        for j in range(4):
            r = m * 4 + j
            for side, buf in ((0, kbuf), (1, vbuf)):
                for slot in range(SLOTS):
                    if slot < SINK_MOST:
                        part = sink[r, slot, side]
                    elif slot == SINK_MOST:
                        part = own[r, side]
                    elif slot < SLOTS - 1:
                        part = win[slot - SINK_MOST - 1, r, side]
                    else:
                        part = kept[r, side]
                    buf[slot * BLK + j * ROWS : slot * BLK + (j + 1) * ROWS, :] = part

        def chunk(i, carry):
            at = pl.multiple_of(i * COLS, COLS)
            here = pl.ds(at, COLS)
            qc, gc = qbuf[here, :], gbuf[here, :]
            scores = []
            for slot in range(SLOTS):
                k = kbuf[slot * BLK : (slot + 1) * BLK, :]
                s = lax.dot_general(k, qc, NT, preferred_element_type=wide) * scale
                if slot == SINK_MOST:
                    u = lax.broadcasted_iota(jnp.int32, (BLK, COLS), 0)
                    t = (lax.broadcasted_iota(jnp.int32, (BLK, COLS), 1) + at) // GROUP
                    s = jnp.where(u <= t, s, -jnp.inf)
                else:
                    s = s + bias[(pair * PAIR + m) * SLOTS + slot]
                scores.append(s)
            top = scores[0]
            for s in scores[1:]:
                top = jnp.maximum(top, s)
            top = jnp.max(top, axis=0, keepdims=True)
            norm = jnp.zeros((BLK, COLS), wide)
            delta = jnp.zeros((BLK, COLS), wide)
            exps, grads = [], []
            for slot in range(SLOTS):
                v = vbuf[slot * BLK : (slot + 1) * BLK, :]
                e = jnp.exp(scores[slot] - top)
                d = lax.dot_general(v, gc, NT, preferred_element_type=wide)
                norm = norm + e
                delta = delta + e * d
                exps.append(e)
                grads.append(d)
            inverse = 1.0 / jnp.sum(norm, axis=0, keepdims=True)
            delta = jnp.sum(delta, axis=0, keepdims=True) * inverse
            for slot in range(SLOTS):
                p = exps[slot] * inverse
                pbuf[slot * BLK : (slot + 1) * BLK, here] = p.astype(low)
                sbuf[slot * BLK : (slot + 1) * BLK, here] = (p * (grads[slot] - delta)).astype(low)
            turned = lax.dot_general(kbuf[...], sbuf[:, here], TN, preferred_element_type=wide)
            tokens = pl.ds(pl.multiple_of(i * (COLS // GROUP), COLS // GROUP), COLS // GROUP)
            dqbuf[tokens, rows, :] = (turned.T * scale).reshape(COLS // GROUP, GROUP, HD)
            return carry

        lax.fori_loop(0, columns // COLS, chunk, 0)

        for slot in range(SLOTS):
            block = slice(slot * BLK, (slot + 1) * BLK)
            dk = lax.dot_general(sbuf[block, :], qbuf[...], NN, preferred_element_type=wide) * scale
            dv = lax.dot_general(pbuf[block, :], gbuf[...], NN, preferred_element_type=wide)
            for j in range(4):
                r = m * 4 + j
                for side, term in ((0, dk), (1, dv)):
                    part = term[j * ROWS : (j + 1) * ROWS]
                    if slot < SINK_MOST:
                        tsink[r, slot, side] = part.astype(low)
                    elif slot < SLOTS - 1:
                        near[slot - SINK_MOST, r, side] = part
                    else:
                        tkept[r, side] = part.astype(low)

    dq[...] = dqbuf[...].astype(low)


def attend(bias, q, g, sink, own, win, kept):
    low, wide = jnp.bfloat16, jnp.float32
    half = N // PAIR
    steps = KVH // PAIR
    tokens = pl.BlockSpec((BLK, PAIR * GROUP, HD), lambda i: (0, i, 0))
    sinks = pl.BlockSpec((half, SINK_MOST) + PIECE, lambda i: (i, 0, 0, 0, 0))
    block = pl.BlockSpec((half,) + PIECE, lambda i: (i, 0, 0, 0))

    def several(count):
        return pl.BlockSpec((count, half) + PIECE, lambda i: (0, i, 0, 0, 0))

    columns = BLK * GROUP
    return pl.pallas_call(
        attend_kernel,
        grid=(steps,),
        out_shape=(
            jax.ShapeDtypeStruct((BLK, KVH * GROUP, HD), low),
            jax.ShapeDtypeStruct((N, SINK_MOST) + PIECE, low),
            jax.ShapeDtypeStruct((N,) + PIECE, low),
            jax.ShapeDtypeStruct((WIN_MOST, N) + PIECE, wide),
        ),
        in_specs=[
            pl.BlockSpec(memory_space=pltpu.SMEM),
            tokens, tokens, sinks, block, several(WIN_MOST - 1), block,
        ],
        out_specs=(tokens, sinks, block, several(WIN_MOST)),
        scratch_shapes=[
            pltpu.VMEM((SLOTS * BLK, HD), low),
            pltpu.VMEM((SLOTS * BLK, HD), low),
            pltpu.VMEM((columns, HD), low),
            pltpu.VMEM((columns, HD), low),
            pltpu.VMEM((SLOTS * BLK, columns), low),
            pltpu.VMEM((SLOTS * BLK, columns), low),
            pltpu.VMEM((BLK, PAIR * GROUP, HD), wide),
        ],
        compiler_params=pltpu.CompilerParams(vmem_limit_bytes=VMEM_LIMIT),
        name="attend",
    )(bias, q, g, sink, own, win, kept)


def tables(kept_blocks, sink_blocks, window_blocks, seq, head):
    lists = lax.dynamic_index_in_dim(kept_blocks[:, :, 0], head // 4, 0, keepdims=False)
    lists = lists.reshape(N, N)
    owners, inner = lists // N, lists % N
    order = jnp.arange(N, dtype=jnp.int32)
    same = owners[:, :, None] == owners[:, None, :]
    ranks = jnp.sum((same & (order[None, :] < order[:, None])[None]).astype(jnp.int32), axis=2)
    places = jnp.arange(CAP, dtype=jnp.int32)
    match = (owners == seq)[:, None, :] & (ranks[:, None, :] == places[None, :, None])
    sent = jnp.sum(jnp.where(match, inner[:, None, :], 0), axis=2).reshape(N * CAP)
    valid = jnp.any(match, axis=2).reshape(N * CAP)
    my_owners = lax.dynamic_index_in_dim(owners, seq, 0, keepdims=False)
    my_ranks = lax.dynamic_index_in_dim(ranks, seq, 0, keepdims=False)
    mine = (my_owners[None, None, :] == order[:, None, None]) & (
        my_ranks[None, None, :] == places[None, :, None]
    )
    fill = N + jnp.sum(jnp.where(mine, order[None, None, :] - N, 0), axis=2).reshape(N * CAP)
    key = jnp.where(valid, sent, N)
    index = jnp.arange(N * CAP, dtype=jnp.int32)
    linked = (key[None, :] == key[:, None]) & (index[None, :] < index[:, None])
    none = N * CAP
    link = jnp.max(jnp.where(linked, index[None, :], -1), axis=1)
    link = jnp.where(link < 0, none, link)
    last = jnp.max(jnp.where(key[None, :] == order[:, None], index[None, :], -1), axis=1)
    last = jnp.where(last < 0, none, last)
    table = jnp.stack(
        [
            sent,
            jnp.concatenate([my_owners, my_ranks]),
            fill,
            link,
            jnp.concatenate([last, last]),
        ]
    )

    current = seq * N + head
    named = lax.dynamic_index_in_dim(kept_blocks[:, :, 0], current, 1, keepdims=True)
    sinks, windows = sink_blocks[:, None], window_blocks[:, None]
    ids = jnp.arange(SINK_MOST, dtype=jnp.int32)[None, :]
    sink_ok = (ids < sinks) & (ids <= current) & (current - ids >= windows)
    back = jnp.arange(WIN_MOST, dtype=jnp.int32)[None, :]
    window_ok = (back < windows) & (current - back >= 0)
    kept_ok = (named <= current) & (named >= sinks) & (current - named >= windows)
    allowed = jnp.concatenate([sink_ok, window_ok, kept_ok], axis=1)
    bias = jnp.where(allowed, 0.0, -jnp.inf).astype(jnp.float32).reshape(KVH * SLOTS)
    return table, bias


def body(queries, keys, values, out_grad, kept_blocks, sink_blocks, window_blocks):
    seq, head = lax.axis_index("seq"), lax.axis_index("head")
    table, bias = tables(kept_blocks, sink_blocks, window_blocks, seq, head)
    pair = jnp.stack([keys, values]).reshape(2, 4, ROWS, KVH, HD)
    own = jnp.transpose(pair, (3, 1, 0, 2, 4)).reshape((N,) + PIECE)
    sink, win, kept = fetch(table, own)
    dq, tsink, tkept, near = attend(bias, queries, out_grad, sink, own, win, kept)
    out = give(table, tsink, tkept, near)
    grads = jnp.transpose(out.reshape(KVH, 4, 2, ROWS, HD), (2, 1, 3, 0, 4))
    grads = grads.reshape(2, BLK, KVH, HD)
    return dq, grads[0], grads[1]


def solution(mesh):
    tokens = P(("dp", "seq", "head"), None, None)
    return jax.shard_map(
        body,
        mesh=mesh,
        in_specs=(tokens, tokens, tokens, tokens, P(), P(), P()),
        out_specs=(tokens, tokens, tokens),
        check_vma=False,
    )
```

```python
import math

import jax
import jax.numpy as jnp
from jax import lax
from jax.experimental import pallas as pl
from jax.experimental.pallas import tpu as pltpu
from jax.sharding import PartitionSpec as P

BLK = 128
SINK_MOST = 3
WIN_MOST = 4
SLOTS = 8
N = 16
KVH = 4
GROUP = 8
HD = 128
CAP = 2
ROWS = 32
PIECE = (2, ROWS, HD)
MESH = pl.DeviceIdType.MESH
VMEM_LIMIT = 60 * 1024 * 1024


def remote(src, dst, send, recv, device):
    return pltpu.make_async_remote_copy(
        src_ref=src, dst_ref=dst, send_sem=send, recv_sem=recv, device_id=device, device_id_type=MESH
    )


def neighbours(seq, head):
    wrap_up = (head == N - 1).astype(jnp.int32)
    wrap_down = (head == 0).astype(jnp.int32)
    after = {"seq": lax.rem(seq + wrap_up, N), "head": lax.rem(head + 1, N)}
    before = {"seq": lax.rem(seq + N - wrap_down, N), "head": lax.rem(head + N - 1, N)}
    return before, after


def greet(seq, head, before, after):
    barrier = pltpu.get_barrier_semaphore()
    for k in range(1, N):
        pl.semaphore_signal(
            barrier, inc=1, device_id={"head": lax.rem(head + k, N)}, device_id_type=MESH
        )
        pl.semaphore_signal(
            barrier, inc=1, device_id={"seq": lax.rem(seq + k, N)}, device_id_type=MESH
        )
    pl.semaphore_signal(barrier, inc=1, device_id=before, device_id_type=MESH)
    pl.semaphore_signal(barrier, inc=1, device_id=after, device_id_type=MESH)
    pl.semaphore_wait(barrier, 2 * (N - 1) + 2)


ORDER = [8] + [k for i in range(1, 8) for k in (i, N - i)]
COLS = 256
COLUMNS = BLK * GROUP
LOWEST = -1e30
NT = (((1,), (1,)), ((), ()))
NN = (((1,), (0,)), ((), ()))
TN = (((0,), (0,)), ((), ()))


def exchange(src, dst, send, recv, me, axis):
    copies = []
    for k in ORDER:
        to = lax.rem(me + k, N)
        copies.append(remote(src.at[to], dst.at[me], send.at[k], recv.at[k], {axis: to}))
        copies[-1].start()
    return copies


def kernel(
    table, bias, q_hbm, g_hbm, own, dq, out,
    rows_in, slots_out, slots_in, far_out, piece, pieces, sink, win, kept,
    tsink, tkept, near, rows, back_out, back_in, run, sums, sums_in,
    sink_in, shares, shares_in, share, whole, hop_out, hop_in, total,
    q_raw, g_raw, qbuf, gbuf, kbuf, ebuf, dbuf, sbuf, efar, dfar, tops, norms, deltas, factors, centre, dqbuf,
    load,
    sw, rw, s1, r1, s2, r2, s3, r3, ss1, rs1, ss2, rs2, ss3, rs3,
    tw, vw, t1, v1, t2, v2, t3, v3, ts1, vs1, ts2, vs2, ts3, vs3,
):
    seq, head = lax.axis_index("seq"), lax.axis_index("head")
    low, wide = jnp.bfloat16, jnp.float32
    scale = 1.0 / math.sqrt(HD)
    before, after = neighbours(seq, head)
    loads = [
        pltpu.make_async_copy(q_hbm, q_raw, load.at[0]),
        pltpu.make_async_copy(g_hbm, g_raw, load.at[1]),
    ]
    for copy in loads:
        copy.start()
    greet(seq, head, before, after)


    def part(ref, g, side):
        return ref[pl.ds(4 * g, 4), side].reshape(BLK, HD)

    def score(g, slot, k, v, e_ref, d_ref):
        kbuf[g, slot * BLK : (slot + 1) * BLK, :] = k
        for i in range(COLUMNS // COLS):
            here = slice(i * COLS, (i + 1) * COLS)
            s = lax.dot_general(k, qbuf[g, here, :], NT, preferred_element_type=wide) * scale
            if slot == SINK_MOST:
                u = lax.broadcasted_iota(jnp.int32, (BLK, COLS), 0)
                t = (lax.broadcasted_iota(jnp.int32, (BLK, COLS), 1) + i * COLS) // GROUP
                s = jnp.where(u <= t, s, -jnp.inf)
            else:
                s = s + bias[g * SLOTS + slot]
            top = jnp.maximum(jnp.max(s, axis=0, keepdims=True), LOWEST)
            e = jnp.exp(s - top)
            d = lax.dot_general(v, gbuf[g, here, :], NT, preferred_element_type=wide)
            e_ref[:, here] = e
            d_ref[:, here] = d
            tops[g, slot : slot + 1, here] = top
            norms[g, slot : slot + 1, here] = jnp.sum(e, axis=0, keepdims=True)
            deltas[g, slot : slot + 1, here] = jnp.sum(e * d, axis=0, keepdims=True)

    def score_all(slot, ref):
        def step(g, carry):
            score(g, slot, part(ref, g, 0), part(ref, g, 1), ebuf.at[g, slot], dbuf.at[g, slot])
            return carry

        lax.fori_loop(0, KVH, step, 0)

    def combine(g):
        t = tops[g]
        w = jnp.exp(t - jnp.max(t, axis=0, keepdims=True))
        inverse = 1.0 / jnp.sum(w * norms[g], axis=0, keepdims=True)
        factors[g] = w * inverse
        centre[g] = jnp.sum(w * deltas[g], axis=0, keepdims=True) * inverse

    def grad(g, slot, e_ref, d_ref, put):
        p = e_ref[...] * factors[g, slot : slot + 1, :]
        ds = (p * (d_ref[...] - centre[g])).astype(low)
        sbuf[g, slot * BLK : (slot + 1) * BLK, :] = ds
        put(0, (lax.dot_general(ds, qbuf[g], NN, preferred_element_type=wide) * scale).reshape(4, ROWS, HD))
        dv = lax.dot_general(p.astype(low), gbuf[g], NN, preferred_element_type=wide)
        put(1, dv.reshape(4, ROWS, HD))

    def grad_all(slot, put):
        def step(g, carry):
            grad(g, slot, ebuf.at[g, slot], dbuf.at[g, slot], lambda side, x: put(pl.ds(4 * g, 4), side, x))
            return carry

        lax.fori_loop(0, KVH, step, 0)


    first = exchange(own, rows_in, s1, r1, head, "head")

    def sink_send(k):
        return remote(own.at[k], piece, ss1.at[k], rs1.at[0], {"seq": k})

    @pl.when((seq == 0) & (head < SINK_MOST))
    def _():
        for k in range(1, N):
            sink_send(k).start()

    steps = [remote(own, win.at[0], sw.at[0], rw.at[0], after)]
    for w in range(1, WIN_MOST - 1):
        steps.append(remote(win.at[w - 1], win.at[w], sw.at[w], rw.at[w], after))
    steps[0].start()
    rows_in[head] = own[head]

    @pl.when((seq == 0) & (head < SINK_MOST))
    def _():
        piece[...] = own[0]

    for copy in loads:
        copy.wait()
    for raw, buf in ((q_raw, qbuf), (g_raw, gbuf)):
        for pair in range(KVH // 2):
            x = raw[:, 16 * pair : 16 * (pair + 1), :].astype(wide)
            for m in range(2):
                buf[2 * pair + m] = x[:, 8 * m : 8 * (m + 1)].reshape(COLUMNS, HD).astype(low)
    score_all(SINK_MOST, own)

    for copy in first:
        copy.wait_recv()
    for k in range(N):
        for c in range(CAP):
            slots_out[k, c] = rows_in[table[0, k * CAP + c]]
    second = exchange(slots_out, slots_in, s2, r2, seq, "seq")
    slots_in[seq] = slots_out[seq]

    def piece_send(k):
        return remote(piece, pieces.at[head], ss2.at[k], rs2.at[head], {"head": lax.rem(head + k, N)})

    @pl.when((seq > 0) & (head < SINK_MOST))
    def _():
        remote(own.at[0], piece, ss1.at[0], rs1.at[0], {"seq": 0}).wait_recv()

    @pl.when(head < SINK_MOST)
    def _():
        for k in ORDER:
            piece_send(k).start()
        pieces[head] = piece[...]

    steps[0].wait_recv()
    steps[1].start()
    score_all(SINK_MOST + 1, win.at[0])

    for copy in second:
        copy.wait_recv()
    for k in range(N):
        far_out[k] = slots_in[table[1, k], table[1, N + k]]
    third = exchange(far_out, kept, s3, r3, head, "head")
    kept[head] = far_out[head]

    steps[1].wait_recv()
    steps[2].start()
    score_all(SINK_MOST + 2, win.at[1])

    for b in range(SINK_MOST):

        @pl.when(head != b)
        def _():
            remote(piece, pieces.at[b], ss2.at[0], rs2.at[b], {"head": b}).wait_recv()

    spread = []
    for k in ORDER:
        to = lax.rem(seq + k, N)
        spread.append(remote(pieces, sink.at[seq], ss3.at[k], rs3.at[k], {"seq": to}))
        spread[-1].start()
    sink[seq] = pieces[...]

    steps[2].wait_recv()
    score_all(SINK_MOST + 3, win.at[2])
    for copy in spread:
        copy.wait_recv()
    for b in range(SINK_MOST):

        def step(g, carry):
            k = sink[pl.ds(4 * g, 4), b, 0].reshape(BLK, HD)
            v = sink[pl.ds(4 * g, 4), b, 1].reshape(BLK, HD)
            score(g, b, k, v, ebuf.at[g, b], dbuf.at[g, b])
            return carry

        lax.fori_loop(0, KVH, step, 0)
    for copy in third:
        copy.wait_recv()


    def kept_step(g, carry):
        score(g, SLOTS - 1, part(kept, g, 0), part(kept, g, 1), efar, dfar)
        combine(g)

        def put(side, x):
            tkept[pl.ds(4 * g, 4), side] = x.astype(low)

        grad(g, SLOTS - 1, efar, dfar, put)
        return carry

    lax.fori_loop(0, KVH, kept_step, 0)
    first_back = exchange(tkept, rows, t1, v1, head, "head")
    rows[head] = tkept[head]
    rows[N] = jnp.zeros(PIECE, low)

    def put_hop(at, side, x):
        hop_out[0, at, side] = x.astype(low)

    grad_all(SLOTS - 2, put_hop)
    hops = [
        remote(hop_out.at[w], hop_in.at[w], tw.at[w], vw.at[w], before) for w in range(WIN_MOST - 1)
    ]
    hops[0].start()

    for b in range(SINK_MOST):

        def put_sink(at, side, x):
            tsink[at, b, side] = x.astype(low)

        grad_all(b, put_sink)
    spread_back = exchange(tsink, sink_in, ts3, vs3, seq, "seq")
    sink_in[seq] = tsink[seq]

    def put_near(n):
        def put(at, side, x):
            near[n, at, side] = x

        return put

    grad_all(SINK_MOST + 2, put_near(2))

    for copy in first_back:
        copy.wait_recv()
    for k in range(N):
        for c in range(CAP):
            back_out[k, c] = rows[table[2, k * CAP + c]]
    second_back = exchange(back_out, back_in, t2, v2, seq, "seq")
    back_in[seq] = back_out[seq]

    hops[0].wait_recv()
    hop_out[1] = (near[2] + hop_in[0].astype(wide)).astype(low)
    hops[1].start()
    grad_all(SINK_MOST + 1, put_near(1))

    for copy in spread_back:
        copy.wait_recv()
    for b in range(SINK_MOST):
        term = sink_in[0, b].astype(wide)
        for k in range(1, N):
            term = term + sink_in[k, b].astype(wide)
        shares[b] = term.astype(low)

    def share_send(b):
        return remote(shares.at[b], shares_in.at[head], ts2.at[b], vs2.at[head], {"head": b})

    for b in range(SINK_MOST):

        @pl.when(head != b)
        def _():
            share_send(b).start()

    run[...] = jnp.zeros(run.shape, wide)
    for copy in second_back:
        copy.wait_recv()
    for k in range(N):
        for c in range(CAP):
            i = k * CAP + c
            run[i] = back_in[k, c].astype(wide) + run[table[3, i]]
    for k in range(N):
        sums[k] = run[table[4, k]].astype(low)
    third_back = exchange(sums, sums_in, t3, v3, head, "head")
    sums_in[head] = sums[head]

    hops[1].wait_recv()
    hop_out[2] = (near[1] + hop_in[1].astype(wide)).astype(low)
    hops[2].start()
    grad_all(SINK_MOST, put_near(0))

    def whole_send():
        return remote(share, whole.at[seq], ts1.at[0], vs1.at[seq], {"seq": 0})

    @pl.when(head < SINK_MOST)
    def _():
        shares_in[head] = shares[head]
        for k in range(1, N):
            frm = lax.rem(head + k, N)
            remote(shares.at[0], shares_in.at[frm], ts2.at[0], vs2.at[frm], {"head": frm}).wait_recv()
        term = shares_in[0].astype(wide)
        for k in range(1, N):
            term = term + shares_in[k].astype(wide)
        share[...] = term.astype(low)

    @pl.when((head < SINK_MOST) & (seq > 0))
    def _():
        whole_send().start()

    for g in range(KVH):
        turned = lax.dot_general(kbuf[g], sbuf[g], TN, preferred_element_type=wide)
        m = g % 2
        dqbuf[:, GROUP * m : GROUP * (m + 1), :] = (turned.T * scale).reshape(BLK, GROUP, HD)
        if m == 1:
            dq[:, GROUP * (g - 1) : GROUP * (g + 1), :] = dqbuf[...].astype(low)

    hops[2].wait_recv()
    total[...] = near[0] + hop_in[2].astype(wide)
    for copy in third_back:
        copy.wait_recv()
    total[...] = total[...] + sums_in[...].astype(wide)

    @pl.when((head < SINK_MOST) & (seq == 0))
    def _():
        whole[0] = share[...]
        for k in range(1, N):
            remote(share, whole.at[k], ts1.at[0], vs1.at[k], {"seq": k}).wait_recv()
        total[...] = total[...] + whole[...].astype(wide)

    out[...] = total[...].astype(low)


    for copy in steps + first + second + third + spread:
        copy.wait_send()
    for copy in hops + first_back + second_back + third_back + spread_back:
        copy.wait_send()

    @pl.when((seq == 0) & (head < SINK_MOST))
    def _():
        for k in range(1, N):
            sink_send(k).wait_send()

    @pl.when(head < SINK_MOST)
    def _():
        for k in ORDER:
            piece_send(k).wait_send()

    for b in range(SINK_MOST):

        @pl.when(head != b)
        def _():
            share_send(b).wait_send()

    @pl.when((head < SINK_MOST) & (seq > 0))
    def _():
        whole_send().wait_send()


def attend(table, bias, q, g, own):
    low, wide = jnp.bfloat16, jnp.float32
    vmem = pl.BlockSpec(memory_space=pltpu.VMEM)
    smem = pl.BlockSpec(memory_space=pltpu.SMEM)
    hbm = pl.BlockSpec(memory_space=pl.ANY)
    dma = pltpu.SemaphoreType.DMA

    def lows(*lead):
        return pltpu.VMEM(lead + PIECE, low)

    def wides(*lead):
        return pltpu.VMEM(lead + PIECE, wide)

    raw = pltpu.VMEM((BLK, KVH * GROUP, HD), low)
    flat = pltpu.VMEM((KVH, COLUMNS, HD), low)
    rows = pltpu.VMEM((KVH, SLOTS, COLUMNS), wide)
    return pl.pallas_call(
        kernel,
        out_shape=(
            jax.ShapeDtypeStruct((BLK, KVH * GROUP, HD), low),
            jax.ShapeDtypeStruct((N,) + PIECE, low),
        ),
        in_specs=[smem, smem, hbm, hbm, vmem],
        out_specs=(vmem, vmem),
        scratch_shapes=[
            lows(N), lows(N, CAP), lows(N, CAP), lows(N), lows(), lows(SINK_MOST),
            lows(N, SINK_MOST), lows(WIN_MOST - 1, N), lows(N),
            lows(N, SINK_MOST), lows(N), wides(WIN_MOST - 1, N), lows(N + 1), lows(N, CAP), lows(N, CAP),
            wides(N * CAP + 1), lows(N), lows(N),
            lows(N, SINK_MOST), lows(SINK_MOST), lows(N), lows(), lows(N),
            lows(WIN_MOST - 1, N), lows(WIN_MOST - 1, N), wides(N),
            raw, raw, flat, flat,
            pltpu.VMEM((KVH, SLOTS * BLK, HD), low),
            pltpu.VMEM((KVH, SLOTS - 1, BLK, COLUMNS), wide),
            pltpu.VMEM((KVH, SLOTS - 1, BLK, COLUMNS), wide),
            pltpu.VMEM((KVH, SLOTS * BLK, COLUMNS), low),
            pltpu.VMEM((BLK, COLUMNS), wide),
            pltpu.VMEM((BLK, COLUMNS), wide),
            rows, rows, rows, rows,
            pltpu.VMEM((KVH, 1, COLUMNS), wide),
            pltpu.VMEM((BLK, 2 * GROUP, HD), wide),
            dma((2,)),
            dma((3,)), dma((3,)), dma((N,)), dma((N,)), dma((N,)), dma((N,)), dma((N,)), dma((N,)),
            dma((N,)), dma((1,)), dma((N,)), dma((N,)), dma((N,)), dma((N,)),
            dma((3,)), dma((3,)), dma((N,)), dma((N,)), dma((N,)), dma((N,)), dma((N,)), dma((N,)),
            dma((1,)), dma((N,)), dma((SINK_MOST,)), dma((N,)), dma((N,)), dma((N,)),
        ],
        compiler_params=pltpu.CompilerParams(
            collective_id=0, has_side_effects=True, vmem_limit_bytes=VMEM_LIMIT
        ),
        name="attend",
    )(table, bias, q, g, own)


def tables(kept_blocks, sink_blocks, window_blocks, seq, head):
    lists = lax.dynamic_index_in_dim(kept_blocks[:, :, 0], head // 4, 0, keepdims=False)
    lists = lists.reshape(N, N)
    owners, inner = lists // N, lists % N
    order = jnp.arange(N, dtype=jnp.int32)
    same = owners[:, :, None] == owners[:, None, :]
    ranks = jnp.sum((same & (order[None, :] < order[:, None])[None]).astype(jnp.int32), axis=2)
    places = jnp.arange(CAP, dtype=jnp.int32)
    match = (owners == seq)[:, None, :] & (ranks[:, None, :] == places[None, :, None])
    sent = jnp.sum(jnp.where(match, inner[:, None, :], 0), axis=2).reshape(N * CAP)
    valid = jnp.any(match, axis=2).reshape(N * CAP)
    my_owners = lax.dynamic_index_in_dim(owners, seq, 0, keepdims=False)
    my_ranks = lax.dynamic_index_in_dim(ranks, seq, 0, keepdims=False)
    mine = (my_owners[None, None, :] == order[:, None, None]) & (
        my_ranks[None, None, :] == places[None, :, None]
    )
    fill = N + jnp.sum(jnp.where(mine, order[None, None, :] - N, 0), axis=2).reshape(N * CAP)
    key = jnp.where(valid, sent, N)
    index = jnp.arange(N * CAP, dtype=jnp.int32)
    linked = (key[None, :] == key[:, None]) & (index[None, :] < index[:, None])
    none = N * CAP
    link = jnp.max(jnp.where(linked, index[None, :], -1), axis=1)
    link = jnp.where(link < 0, none, link)
    last = jnp.max(jnp.where(key[None, :] == order[:, None], index[None, :], -1), axis=1)
    last = jnp.where(last < 0, none, last)
    table = jnp.stack(
        [
            sent,
            jnp.concatenate([my_owners, my_ranks]),
            fill,
            link,
            jnp.concatenate([last, last]),
        ]
    )

    current = seq * N + head
    named = lax.dynamic_index_in_dim(kept_blocks[:, :, 0], current, 1, keepdims=True)
    sinks, windows = sink_blocks[:, None], window_blocks[:, None]
    ids = jnp.arange(SINK_MOST, dtype=jnp.int32)[None, :]
    sink_ok = (ids < sinks) & (ids <= current) & (current - ids >= windows)
    back = jnp.arange(WIN_MOST, dtype=jnp.int32)[None, :]
    window_ok = (back < windows) & (current - back >= 0)
    kept_ok = (named <= current) & (named >= sinks) & (current - named >= windows)
    allowed = jnp.concatenate([sink_ok, window_ok, kept_ok], axis=1)
    bias = jnp.where(allowed, 0.0, -jnp.inf).astype(jnp.float32).reshape(KVH * SLOTS)
    return table, bias


def body(queries, keys, values, out_grad, kept_blocks, sink_blocks, window_blocks):
    seq, head = lax.axis_index("seq"), lax.axis_index("head")
    table, bias = tables(kept_blocks, sink_blocks, window_blocks, seq, head)
    pair = jnp.stack([keys, values]).reshape(2, 4, ROWS, KVH, HD)
    own = jnp.transpose(pair, (3, 1, 0, 2, 4)).reshape((N,) + PIECE)
    dq, out = attend(table, bias, queries, out_grad, own)
    grads = jnp.transpose(out.reshape(KVH, 4, 2, ROWS, HD), (2, 1, 3, 0, 4))
    grads = grads.reshape(2, BLK, KVH, HD)
    return dq, grads[0], grads[1]


def solution(mesh):
    tokens = P(("dp", "seq", "head"), None, None)
    return jax.shard_map(
        body,
        mesh=mesh,
        in_specs=(tokens, tokens, tokens, tokens, P(), P(), P()),
        out_specs=(tokens, tokens, tokens),
        check_vma=False,
    )
```

```python
import math

import jax
import jax.numpy as jnp
from jax import lax
from jax.experimental import pallas as pl
from jax.experimental.pallas import tpu as pltpu
from jax.sharding import PartitionSpec as P

BLK = 128
SINK_MOST = 3
WIN_MOST = 4
SLOTS = 8
N = 16
KVH = 4
GROUP = 8
HD = 128
CAP = 2
ROWS = 32
PIECE = (2, ROWS, HD)
MESH = pl.DeviceIdType.MESH
VMEM_LIMIT = 60 * 1024 * 1024


def remote(src, dst, send, recv, device):
    return pltpu.make_async_remote_copy(
        src_ref=src, dst_ref=dst, send_sem=send, recv_sem=recv, device_id=device, device_id_type=MESH
    )


def neighbours(seq, head):
    wrap_up = (head == N - 1).astype(jnp.int32)
    wrap_down = (head == 0).astype(jnp.int32)
    after = {"seq": lax.rem(seq + wrap_up, N), "head": lax.rem(head + 1, N)}
    before = {"seq": lax.rem(seq + N - wrap_down, N), "head": lax.rem(head + N - 1, N)}
    return before, after


def greet(seq, head, before, after):
    barrier = pltpu.get_barrier_semaphore()
    for k in range(1, N):
        pl.semaphore_signal(
            barrier, inc=1, device_id={"head": lax.rem(head + k, N)}, device_id_type=MESH
        )
        pl.semaphore_signal(
            barrier, inc=1, device_id={"seq": lax.rem(seq + k, N)}, device_id_type=MESH
        )
    pl.semaphore_signal(barrier, inc=1, device_id=before, device_id_type=MESH)
    pl.semaphore_signal(barrier, inc=1, device_id=after, device_id_type=MESH)
    pl.semaphore_wait(barrier, 2 * (N - 1) + 2)


ORDER = [8] + [k for i in range(1, 8) for k in (i, N - i)]
COLS = 256
CHUNKS = 2
NEAR = (2, 1, N - 1)
COLUMNS = BLK * GROUP
LOWEST = -1e30
NT = (((1,), (1,)), ((), ()))
NN = (((1,), (0,)), ((), ()))
TN = (((0,), (0,)), ((), ()))


def exchange(src, dst, send, recv, me, axis):
    copies = []
    for k in ORDER:
        to = lax.rem(me + k, N)
        copies.append(remote(src.at[to], dst.at[me], send.at[k], recv.at[k], {axis: to}))
        copies[-1].start()
    return copies


def kernel(
    kept_blocks, sink_blocks, window_blocks, q_hbm, g_hbm, keys, values, dq, dk, dv,
    own, rows_in, slots_out, slots_in, far_out, piece, pieces, sink, win, kept,
    tsink, tkept, near, rows, back_out, back_in, run, sums, sums_in,
    sink_in, shares, shares_in, shares_far, share, whole_out, whole, hop_out, hop_in, total,
    q_raw, g_raw, qbuf, gbuf, kbuf, ebuf, dbuf, sbuf, efar, dfar, tops, norms, deltas, factors, centre, dqbuf,
    marks, fills, links, lasts, load,
    sw, rw, s1, r1, s2, r2, s3, r3, ss1, rs1, ss2, rs2, ss3, rs3,
    tw, vw, t1, v1, t2, v2, t3, v3, ts1, vs1, ts2, vs2, ts3, vs3,
):
    seq, head = lax.axis_index("seq"), lax.axis_index("head")
    low, wide = jnp.bfloat16, jnp.float32
    scale = 1.0 / math.sqrt(HD)
    before, after = neighbours(seq, head)
    loads = [
        pltpu.make_async_copy(q_hbm, q_raw, load.at[0]),
        pltpu.make_async_copy(g_hbm, g_raw, load.at[1]),
    ]
    for copy in loads:
        copy.start()
    for side, ref in ((0, keys), (1, values)):
        x = ref[...].astype(wide)
        for g in range(KVH):
            own[4 * g : 4 * (g + 1), side] = x[:, g, :].astype(low).reshape(4, ROWS, HD)
    greet(seq, head, before, after)


    current = seq * N + head

    def allowed(g, slot):
        sinks, windows = sink_blocks[g], window_blocks[g]
        if slot < SINK_MOST:
            return (slot < sinks) & (slot <= current) & (current - slot >= windows)
        if slot < SLOTS - 1:
            return (slot - SINK_MOST < windows) & (slot - SINK_MOST <= current)
        named = kept_blocks[g, current]
        return (named <= current) & (named >= sinks) & (current - named >= windows)

    def part(ref, g, side):
        return ref[pl.ds(4 * g, 4), side].reshape(BLK, HD)

    def score(g, slot, k, v, e_ref, d_ref):
        kbuf[g, slot * BLK : (slot + 1) * BLK, :] = k
        bias = jnp.where(allowed(g, slot), 0.0, -jnp.inf)
        for i in range(COLUMNS // COLS):
            here = slice(i * COLS, (i + 1) * COLS)
            s = lax.dot_general(k, qbuf[g, here, :], NT, preferred_element_type=wide) * scale
            if slot == SINK_MOST:
                u = lax.broadcasted_iota(jnp.int32, (BLK, COLS), 0)
                t = (lax.broadcasted_iota(jnp.int32, (BLK, COLS), 1) + i * COLS) // GROUP
                s = jnp.where(u <= t, s, -jnp.inf)
            else:
                s = s + bias
            top = jnp.maximum(jnp.max(s, axis=0, keepdims=True), LOWEST)
            e = jnp.exp(s - top)
            d = lax.dot_general(v, gbuf[g, here, :], NT, preferred_element_type=wide)
            e_ref[:, here] = e
            d_ref[:, here] = d
            tops[g, slot : slot + 1, here] = top
            norms[g, slot : slot + 1, here] = jnp.sum(e, axis=0, keepdims=True)
            deltas[g, slot : slot + 1, here] = jnp.sum(e * d, axis=0, keepdims=True)

    def score_all(slot, ref):
        def step(g, carry):
            score(g, slot, part(ref, g, 0), part(ref, g, 1), ebuf.at[g, slot], dbuf.at[g, slot])
            return carry

        lax.fori_loop(0, KVH, step, 0)

    def combine(g):
        t = tops[g]
        w = jnp.exp(t - jnp.max(t, axis=0, keepdims=True))
        inverse = 1.0 / jnp.sum(w * norms[g], axis=0, keepdims=True)
        factors[g] = w * inverse
        centre[g] = jnp.sum(w * deltas[g], axis=0, keepdims=True) * inverse

    def grad(g, slot, e_ref, d_ref, put):
        p = e_ref[...] * factors[g, slot : slot + 1, :]
        ds = (p * (d_ref[...] - centre[g])).astype(low)
        sbuf[g, slot * BLK : (slot + 1) * BLK, :] = ds
        put(0, (lax.dot_general(ds, qbuf[g], NN, preferred_element_type=wide) * scale).reshape(4, ROWS, HD))
        dv = lax.dot_general(p.astype(low), gbuf[g], NN, preferred_element_type=wide)
        put(1, dv.reshape(4, ROWS, HD))

    def grad_all(slot, put):
        def step(g, carry):
            grad(g, slot, ebuf.at[g, slot], dbuf.at[g, slot], lambda side, x: put(pl.ds(4 * g, 4), side, x))
            return carry

        lax.fori_loop(0, KVH, step, 0)


    group = head // 4
    nowhere = N * CAP

    def mark(d, carry):
        first, second = jnp.int32(N), jnp.int32(N)
        for p in range(N):
            entry = kept_blocks[group, d * N + p]
            inner = jnp.where((entry >> 4) == seq, entry & (N - 1), N)
            second = jnp.where(first < N, jnp.where(second < N, second, inner), second)
            first = jnp.where(first < N, first, inner)
        marks[CAP * d] = first
        marks[CAP * d + 1] = second
        return carry

    def places():
        owners = [kept_blocks[group, seq * N + p] >> 4 for p in range(N)]
        found = []
        for p in range(N):
            rank = jnp.int32(0)
            for r in range(p):
                rank = rank + jnp.where(owners[r] == owners[p], 1, 0)
            found.append(CAP * owners[p] + rank)
        return found

    def fill(i, carry):
        which = jnp.int32(N)
        for p in range(N):
            which = jnp.where(slot_of[p] == i, p, which)
        fills[i] = which
        return carry

    def link(i, carry):
        which, key = jnp.int32(nowhere), marks[i]
        for r in range(N * CAP):
            which = jnp.where((marks[r] == key) & (r < i), r, which)
        links[i] = which
        return carry

    def last(z, carry):
        which = jnp.int32(nowhere)
        for r in range(N * CAP):
            which = jnp.where(marks[r] == z, r, which)
        lasts[z] = which
        return carry


    first = exchange(own, rows_in, s1, r1, head, "head")

    def sink_send(k):
        return remote(own.at[k], piece, ss1.at[k], rs1.at[0], {"seq": k})

    @pl.when((seq == 0) & (head < SINK_MOST))
    def _():
        for k in range(1, N):
            sink_send(k).start()

    steps = []

    def relay(w):
        for c in range(CHUNKS):
            at = pl.ds(c * (N // CHUNKS), N // CHUNKS)
            i = w * CHUNKS + c
            src = own.at[at] if w == 0 else win.at[w - 1, at]
            if w > 0:
                steps[i - CHUNKS].wait_recv()
            steps.append(remote(src, win.at[w, at], sw.at[i], rw.at[i], after))
            steps[i].start()

    relay(0)
    rows_in[head] = own[head]

    @pl.when((seq == 0) & (head < SINK_MOST))
    def _():
        piece[...] = own[0]

    for copy in loads:
        copy.wait()
    for raw, buf in ((q_raw, qbuf), (g_raw, gbuf)):
        for pair in range(KVH // 2):
            x = raw[:, 16 * pair : 16 * (pair + 1), :].astype(wide)
            for m in range(2):
                buf[2 * pair + m] = x[:, 8 * m : 8 * (m + 1)].reshape(COLUMNS, HD).astype(low)
    mine = lax.rem(head, 4)

    def piece_far(k):
        return remote(piece, pieces.at[mine], ss2.at[k], rs2.at[mine], {"head": lax.rem(head + 4 * k, N)})

    def piece_near(k):
        to = lax.rem(head + k, N)
        return remote(pieces.at[mine], pieces.at[mine], ss2.at[k], rs2.at[mine], {"head": to})

    lax.fori_loop(0, N, mark, 0)
    score_all(SINK_MOST, own)

    @pl.when((seq > 0) & (head < SINK_MOST))
    def _():
        remote(own.at[0], piece, ss1.at[0], rs1.at[0], {"seq": 0}).wait_recv()

    @pl.when(head < SINK_MOST)
    def _():
        for k in (2, 1, 3):
            piece_far(k).start()
        pieces[head] = piece[...]

    for copy in first:
        copy.wait_recv()
    for k in range(N):
        for c in range(CAP):
            slots_out[k, c] = rows_in[jnp.minimum(marks[k * CAP + c], N - 1)]
    second = exchange(slots_out, slots_in, s2, r2, seq, "seq")
    slots_in[seq] = slots_out[seq]

    relay(1)
    score_all(SINK_MOST + 1, win.at[0])
    slot_of = places()

    @pl.when((mine < SINK_MOST) & (head >= SINK_MOST))
    def _():
        remote(piece, pieces.at[mine], ss2.at[0], rs2.at[mine], {"head": mine}).wait_recv()

    @pl.when(mine < SINK_MOST)
    def _():
        for k in NEAR:
            piece_near(k).start()

    for copy in second:
        copy.wait_recv()
    for k in range(N):
        far_out[k] = slots_in[slot_of[k] >> 1, slot_of[k] & 1]
    third = exchange(far_out, kept, s3, r3, head, "head")
    kept[head] = far_out[head]

    for b in range(SINK_MOST):

        @pl.when(mine != b)
        def _():
            remote(piece, pieces.at[b], ss2.at[0], rs2.at[b], {"head": b}).wait_recv()

    spread = []
    for k in ORDER:
        to = lax.rem(seq + k, N)
        spread.append(remote(pieces, sink.at[seq], ss3.at[k], rs3.at[k], {"seq": to}))
        spread[-1].start()
    sink[seq] = pieces[...]

    relay(2)
    score_all(SINK_MOST + 2, win.at[1])

    for copy in steps[2 * CHUNKS :]:
        copy.wait_recv()
    score_all(SINK_MOST + 3, win.at[2])
    for copy in spread:
        copy.wait_recv()
    for b in range(SINK_MOST):

        def step(g, carry):
            k = sink[pl.ds(4 * g, 4), b, 0].reshape(BLK, HD)
            v = sink[pl.ds(4 * g, 4), b, 1].reshape(BLK, HD)
            score(g, b, k, v, ebuf.at[g, b], dbuf.at[g, b])
            return carry

        lax.fori_loop(0, KVH, step, 0)
    for copy in third:
        copy.wait_recv()


    def kept_step(g, carry):
        score(g, SLOTS - 1, part(kept, g, 0), part(kept, g, 1), efar, dfar)
        combine(g)

        def put(side, x):
            tkept[pl.ds(4 * g, 4), side] = x.astype(low)

        grad(g, SLOTS - 1, efar, dfar, put)
        return carry

    lax.fori_loop(0, KVH, kept_step, 0, unroll=True)
    first_back = exchange(tkept, rows, t1, v1, head, "head")
    rows[head] = tkept[head]
    rows[N] = jnp.zeros(PIECE, low)

    for b in range(SINK_MOST):

        def put_sink(at, side, x):
            tsink[at, b, side] = x.astype(low)

        grad_all(b, put_sink)
    spread_back = exchange(tsink, sink_in, ts3, vs3, seq, "seq")
    sink_in[seq] = tsink[seq]

    def put_hop(at, side, x):
        hop_out[0, at, side] = x.astype(low)

    grad_all(SLOTS - 2, put_hop)
    hops = []

    def hop(w):
        for c in range(CHUNKS):
            at = pl.ds(c * (N // CHUNKS), N // CHUNKS)
            i = w * CHUNKS + c
            if w > 0:
                hops[i - CHUNKS].wait_recv()
                hop_out[w, at] = (near[WIN_MOST - 1 - w, at] + hop_in[w - 1, at].astype(wide)).astype(low)
            hops.append(remote(hop_out.at[w, at], hop_in.at[w, at], tw.at[i], vw.at[i], before))
            hops[i].start()

    hop(0)
    lax.fori_loop(0, N * CAP, fill, 0)

    def put_near(n):
        def put(at, side, x):
            near[n, at, side] = x

        return put

    grad_all(SINK_MOST + 2, put_near(2))

    for copy in first_back:
        copy.wait_recv()
    for k in range(N):
        for c in range(CAP):
            back_out[k, c] = rows[fills[k * CAP + c]]
    second_back = exchange(back_out, back_in, t2, v2, seq, "seq")
    back_in[seq] = back_out[seq]

    for copy in spread_back:
        copy.wait_recv()
    for b in range(SINK_MOST):
        term = sink_in[0, b].astype(wide)
        for k in range(1, N):
            term = term + sink_in[k, b].astype(wide)
        shares[b] = term.astype(low)

    def share_near(b):
        r = lax.rem(head + 4 - b, 4)
        to = lax.rem(jnp.where(r == 3, head + 1, head + N - r), N)
        return remote(shares.at[b], shares_in.at[r], ts2.at[b], vs2.at[r], {"head": to})

    for b in range(SINK_MOST):

        @pl.when(mine != b)
        def _():
            share_near(b).start()

    hop(1)
    grad_all(SINK_MOST + 1, put_near(1))

    def share_far():
        k = 3 + head // 4
        return remote(share, shares_far.at[k - 4], ts2.at[3], vs2.at[k], {"head": mine})

    @pl.when(mine < SINK_MOST)
    def _():
        term = shares[mine].astype(wide)
        for k in range(1, 4):
            remote(shares.at[0], shares_in.at[k], ts2.at[3], vs2.at[k], {"head": mine}).wait_recv()
            term = term + shares_in[k].astype(wide)
        share[...] = term

    @pl.when((mine < SINK_MOST) & (head >= SINK_MOST))
    def _():
        share_far().start()

    lax.fori_loop(0, N * CAP, link, 0)
    lax.fori_loop(0, N, last, 0)
    run[...] = jnp.zeros(run.shape, wide)

    for copy in second_back:
        copy.wait_recv()
    for k in range(N):
        for c in range(CAP):
            i = k * CAP + c
            run[i] = back_in[k, c].astype(wide) + run[links[i]]
    for k in range(N):
        sums[k] = run[lasts[k]].astype(low)
    third_back = exchange(sums, sums_in, t3, v3, head, "head")
    sums_in[head] = sums[head]

    hop(2)

    grad_all(SINK_MOST, put_near(0))

    for g in range(KVH):
        turned = lax.dot_general(kbuf[g], sbuf[g], TN, preferred_element_type=wide)
        m = g % 2
        dqbuf[:, GROUP * m : GROUP * (m + 1), :] = (turned.T * scale).reshape(BLK, GROUP, HD)
        if m == 1:
            dq[:, GROUP * (g - 1) : GROUP * (g + 1), :] = dqbuf[...].astype(low)

    def whole_send():
        return remote(whole_out, whole.at[seq], ts1.at[0], vs1.at[seq], {"seq": 0})

    @pl.when(head < SINK_MOST)
    def _():
        term = share[...]
        for k in range(4, 7):
            remote(share, shares_far.at[k - 4], ts2.at[3], vs2.at[k], {"head": mine}).wait_recv()
            term = term + shares_far[k - 4]
        whole_out[...] = term

    @pl.when((head < SINK_MOST) & (seq > 0))
    def _():
        whole_send().start()

    for copy in hops[2 * CHUNKS :]:
        copy.wait_recv()
    total[...] = near[0] + hop_in[2].astype(wide)
    for copy in third_back:
        copy.wait_recv()
    total[...] = total[...] + sums_in[...].astype(wide)

    @pl.when((head < SINK_MOST) & (seq == 0))
    def _():
        whole[0] = whole_out[...]
        for k in range(1, N):
            remote(whole_out, whole.at[k], ts1.at[0], vs1.at[k], {"seq": k}).wait_recv()
        total[...] = total[...] + whole[...]

    for side, ref in ((0, dk), (1, dv)):
        heads = [total[4 * g : 4 * (g + 1), side].reshape(BLK, HD) for g in range(KVH)]
        ref[...] = jnp.stack(heads, axis=1).astype(low)


    for copy in steps + first + second + third + spread:
        copy.wait_send()
    for copy in hops + first_back + second_back + third_back + spread_back:
        copy.wait_send()

    @pl.when((seq == 0) & (head < SINK_MOST))
    def _():
        for k in range(1, N):
            sink_send(k).wait_send()

    @pl.when(head < SINK_MOST)
    def _():
        for k in (2, 1, 3):
            piece_far(k).wait_send()

    @pl.when(mine < SINK_MOST)
    def _():
        for k in NEAR:
            piece_near(k).wait_send()

    for b in range(SINK_MOST):

        @pl.when(mine != b)
        def _():
            share_near(b).wait_send()

    @pl.when((mine < SINK_MOST) & (head >= SINK_MOST))
    def _():
        share_far().wait_send()

    @pl.when((head < SINK_MOST) & (seq > 0))
    def _():
        whole_send().wait_send()


def attend(kept_blocks, sink_blocks, window_blocks, q, g, keys, values):
    low, wide = jnp.bfloat16, jnp.float32
    vmem = pl.BlockSpec(memory_space=pltpu.VMEM)
    smem = pl.BlockSpec(memory_space=pltpu.SMEM)
    hbm = pl.BlockSpec(memory_space=pl.ANY)
    dma = pltpu.SemaphoreType.DMA

    def lows(*lead):
        return pltpu.VMEM(lead + PIECE, low)

    def wides(*lead):
        return pltpu.VMEM(lead + PIECE, wide)

    raw = pltpu.VMEM((BLK, KVH * GROUP, HD), low)
    flat = pltpu.VMEM((KVH, COLUMNS, HD), low)
    rows = pltpu.VMEM((KVH, SLOTS, COLUMNS), wide)
    return pl.pallas_call(
        kernel,
        out_shape=(
            jax.ShapeDtypeStruct((BLK, KVH * GROUP, HD), low),
            jax.ShapeDtypeStruct((BLK, KVH, HD), low),
            jax.ShapeDtypeStruct((BLK, KVH, HD), low),
        ),
        in_specs=[smem, smem, smem, hbm, hbm, vmem, vmem],
        out_specs=(vmem, vmem, vmem),
        scratch_shapes=[
            lows(N),
            lows(N), lows(N, CAP), lows(N, CAP), lows(N), lows(), lows(SINK_MOST),
            lows(N, SINK_MOST), lows(WIN_MOST - 1, N), lows(N),
            lows(N, SINK_MOST), lows(N), wides(WIN_MOST - 1, N), lows(N + 1), lows(N, CAP), lows(N, CAP),
            wides(N * CAP + 1), lows(N), lows(N),
            lows(N, SINK_MOST), lows(SINK_MOST), lows(4), wides(3), wides(), wides(), wides(N),
            lows(WIN_MOST - 1, N), lows(WIN_MOST - 1, N), wides(N),
            raw, raw, flat, flat,
            pltpu.VMEM((KVH, SLOTS * BLK, HD), low),
            pltpu.VMEM((KVH, SLOTS - 1, BLK, COLUMNS), wide),
            pltpu.VMEM((KVH, SLOTS - 1, BLK, COLUMNS), wide),
            pltpu.VMEM((KVH, SLOTS * BLK, COLUMNS), low),
            pltpu.VMEM((BLK, COLUMNS), wide),
            pltpu.VMEM((BLK, COLUMNS), wide),
            rows, rows, rows, rows,
            pltpu.VMEM((KVH, 1, COLUMNS), wide),
            pltpu.VMEM((BLK, 2 * GROUP, HD), wide),
            pltpu.SMEM((N * CAP,), jnp.int32), pltpu.SMEM((N * CAP,), jnp.int32),
            pltpu.SMEM((N * CAP,), jnp.int32), pltpu.SMEM((N,), jnp.int32),
            dma((2,)),
            dma((3 * CHUNKS,)), dma((3 * CHUNKS,)), dma((N,)), dma((N,)), dma((N,)), dma((N,)), dma((N,)), dma((N,)),
            dma((N,)), dma((1,)), dma((N,)), dma((N,)), dma((N,)), dma((N,)),
            dma((3 * CHUNKS,)), dma((3 * CHUNKS,)), dma((N,)), dma((N,)), dma((N,)), dma((N,)), dma((N,)), dma((N,)),
            dma((1,)), dma((N,)), dma((4,)), dma((8,)), dma((N,)), dma((N,)),
        ],
        compiler_params=pltpu.CompilerParams(
            collective_id=0, has_side_effects=True, vmem_limit_bytes=VMEM_LIMIT
        ),
        name="attend",
    )(kept_blocks, sink_blocks, window_blocks, q, g, keys, values)


def body(queries, keys, values, out_grad, kept_blocks, sink_blocks, window_blocks):
    lists = kept_blocks.reshape(KVH, N * N)
    return attend(lists, sink_blocks, window_blocks, queries, out_grad, keys, values)


def solution(mesh):
    tokens = P(("dp", "seq", "head"), None, None)
    return jax.shard_map(
        body,
        mesh=mesh,
        in_specs=(tokens, tokens, tokens, tokens, P(), P(), P()),
        out_specs=(tokens, tokens, tokens),
        check_vma=False,
    )
```

```python
import math

import jax
import jax.numpy as jnp
from jax import lax
from jax.experimental import pallas as pl
from jax.experimental.pallas import tpu as pltpu
from jax.sharding import PartitionSpec as P

BLK = 128
SINK_MOST = 3
WIN_MOST = 4
SLOTS = 8
N = 16
KVH = 4
GROUP = 8
HD = 128
CAP = 2
ROWS = 32
PIECE = (2, ROWS, HD)
MESH = pl.DeviceIdType.MESH
VMEM_LIMIT = 60 * 1024 * 1024


def remote(src, dst, send, recv, device):
    return pltpu.make_async_remote_copy(
        src_ref=src, dst_ref=dst, send_sem=send, recv_sem=recv, device_id=device, device_id_type=MESH
    )


def neighbours(seq, head):
    wrap_up = (head == N - 1).astype(jnp.int32)
    wrap_down = (head == 0).astype(jnp.int32)
    after = {"seq": lax.rem(seq + wrap_up, N), "head": lax.rem(head + 1, N)}
    before = {"seq": lax.rem(seq + N - wrap_down, N), "head": lax.rem(head + N - 1, N)}
    return before, after


def greet(seq, head, before, after):
    barrier = pltpu.get_barrier_semaphore()
    for k in range(1, N):
        pl.semaphore_signal(
            barrier, inc=1, device_id={"head": lax.rem(head + k, N)}, device_id_type=MESH
        )
        pl.semaphore_signal(
            barrier, inc=1, device_id={"seq": lax.rem(seq + k, N)}, device_id_type=MESH
        )
    pl.semaphore_signal(barrier, inc=1, device_id=before, device_id_type=MESH)
    pl.semaphore_signal(barrier, inc=1, device_id=after, device_id_type=MESH)
    pl.semaphore_wait(barrier, 2 * (N - 1) + 2)


ORDER = [8] + [k for i in range(1, 8) for k in (i, N - i)]
COLS = 256
CHUNKS = 2
NEAR = (2, 1, N - 1)
COLUMNS = BLK * GROUP
LOWEST = -1e30
NT = (((1,), (1,)), ((), ()))
NN = (((1,), (0,)), ((), ()))
TN = (((0,), (0,)), ((), ()))


def exchange(src, dst, send, recv, me, axis):
    copies = []
    for k in ORDER:
        to = lax.rem(me + k, N)
        copies.append(remote(src.at[to], dst.at[me], send.at[k], recv.at[k], {axis: to}))
        copies[-1].start()
    return copies


def kernel(
    kept_blocks, sink_blocks, window_blocks, q_hbm, g_hbm, keys, values, dq, dk, dv,
    own, rows_in, slots_out, slots_in, far_out, piece, pieces, sink, win, kept,
    tsink, tkept, near, rows, back_out, back_in, run, sums, sums_in,
    sink_in, shares, shares_in, shares_far, share, whole_out, whole, hop_out, hop_in, total,
    q_raw, g_raw, qbuf, gbuf, kbuf, ebuf, dbuf, sbuf, efar, dfar, tops, norms, deltas, factors, centre, dqbuf,
    marks, fills, links, lasts, load,
    sw, rw, s1, r1, s2, r2, s3, r3, ss1, rs1, ss2, rs2, ss3, rs3,
    tw, vw, t1, v1, t2, v2, t3, v3, ts1, vs1, ts2, vs2, ts3, vs3,
):
    seq, head = lax.axis_index("seq"), lax.axis_index("head")
    low, wide = jnp.bfloat16, jnp.float32
    scale = 1.0 / math.sqrt(HD)
    before, after = neighbours(seq, head)
    loads = [
        pltpu.make_async_copy(q_hbm, q_raw, load.at[0]),
        pltpu.make_async_copy(g_hbm, g_raw, load.at[1]),
    ]
    for copy in loads:
        copy.start()
    for side, ref in ((0, keys), (1, values)):
        x = ref[...].astype(wide)
        for g in range(KVH):
            own[4 * g : 4 * (g + 1), side] = x[:, g, :].astype(low).reshape(4, ROWS, HD)
    greet(seq, head, before, after)


    current = seq * N + head

    def allowed(g, slot):
        sinks, windows = sink_blocks[g], window_blocks[g]
        if slot < SINK_MOST:
            return (slot < sinks) & (slot <= current) & (current - slot >= windows)
        if slot < SLOTS - 1:
            return (slot - SINK_MOST < windows) & (slot - SINK_MOST <= current)
        named = kept_blocks[g, current]
        return (named <= current) & (named >= sinks) & (current - named >= windows)

    def part(ref, g, side):
        return ref[pl.ds(4 * g, 4), side].reshape(BLK, HD)

    def score(g, slot, k, v, e_ref, d_ref):
        kbuf[g, slot * BLK : (slot + 1) * BLK, :] = k
        bias = jnp.where(allowed(g, slot), 0.0, -jnp.inf)
        for i in range(COLUMNS // COLS):
            here = slice(i * COLS, (i + 1) * COLS)
            s = lax.dot_general(k, qbuf[g, here, :], NT, preferred_element_type=wide) * scale
            if slot == SINK_MOST:
                u = lax.broadcasted_iota(jnp.int32, (BLK, COLS), 0)
                t = (lax.broadcasted_iota(jnp.int32, (BLK, COLS), 1) + i * COLS) // GROUP
                s = jnp.where(u <= t, s, -jnp.inf)
            else:
                s = s + bias
            top = jnp.maximum(jnp.max(s, axis=0, keepdims=True), LOWEST)
            e = jnp.exp(s - top)
            d = lax.dot_general(v, gbuf[g, here, :], NT, preferred_element_type=wide)
            e_ref[:, here] = e
            d_ref[:, here] = d
            tops[g, slot : slot + 1, here] = top
            norms[g, slot : slot + 1, here] = jnp.sum(e, axis=0, keepdims=True)
            deltas[g, slot : slot + 1, here] = jnp.sum(e * d, axis=0, keepdims=True)

    def score_all(slot, ref):
        def step(g, carry):
            score(g, slot, part(ref, g, 0), part(ref, g, 1), ebuf.at[g, slot], dbuf.at[g, slot])
            return carry

        lax.fori_loop(0, KVH, step, 0)

    def score_sinks(g, carry):
        k = jnp.concatenate([sink[pl.ds(4 * g, 4), b, 0].reshape(BLK, HD) for b in range(SINK_MOST)])
        v = jnp.concatenate([sink[pl.ds(4 * g, 4), b, 1].reshape(BLK, HD) for b in range(SINK_MOST)])
        kbuf[g, : SINK_MOST * BLK, :] = k
        biases = [jnp.where(allowed(g, b), 0.0, -jnp.inf) for b in range(SINK_MOST)]
        for i in range(COLUMNS // COLS):
            here = slice(i * COLS, (i + 1) * COLS)
            s = lax.dot_general(k, qbuf[g, here, :], NT, preferred_element_type=wide) * scale
            d = lax.dot_general(v, gbuf[g, here, :], NT, preferred_element_type=wide)
            for b in range(SINK_MOST):
                rows_b = slice(b * BLK, (b + 1) * BLK)
                t = s[rows_b] + biases[b]
                top = jnp.maximum(jnp.max(t, axis=0, keepdims=True), LOWEST)
                e = jnp.exp(t - top)
                ebuf[g, b, :, here] = e
                dbuf[g, b, :, here] = d[rows_b]
                tops[g, b : b + 1, here] = top
                norms[g, b : b + 1, here] = jnp.sum(e, axis=0, keepdims=True)
                deltas[g, b : b + 1, here] = jnp.sum(e * d[rows_b], axis=0, keepdims=True)
        return carry

    def combine(g):
        t = tops[g]
        w = jnp.exp(t - jnp.max(t, axis=0, keepdims=True))
        inverse = 1.0 / jnp.sum(w * norms[g], axis=0, keepdims=True)
        factors[g] = w * inverse
        centre[g] = jnp.sum(w * deltas[g], axis=0, keepdims=True) * inverse

    def grad(g, slot, e_ref, d_ref, put):
        p = e_ref[...] * factors[g, slot : slot + 1, :]
        ds = (p * (d_ref[...] - centre[g])).astype(low)
        sbuf[g, slot * BLK : (slot + 1) * BLK, :] = ds
        put(0, (lax.dot_general(ds, qbuf[g], NN, preferred_element_type=wide) * scale).reshape(4, ROWS, HD))
        dv = lax.dot_general(p.astype(low), gbuf[g], NN, preferred_element_type=wide)
        put(1, dv.reshape(4, ROWS, HD))

    def grad_sinks(g, carry):
        terms = []
        for b in range(SINK_MOST):
            p = ebuf[g, b] * factors[g, b : b + 1, :]
            terms.append((p.astype(low), (p * (dbuf[g, b] - centre[g])).astype(low)))
        p = jnp.concatenate([t[0] for t in terms])
        ds = jnp.concatenate([t[1] for t in terms])
        sbuf[g, : SINK_MOST * BLK, :] = ds
        dk = lax.dot_general(ds, qbuf[g], NN, preferred_element_type=wide) * scale
        dv = lax.dot_general(p, gbuf[g], NN, preferred_element_type=wide)
        for b in range(SINK_MOST):
            for side, x in ((0, dk), (1, dv)):
                part_b = x[b * BLK : (b + 1) * BLK].reshape(4, ROWS, HD)
                tsink[pl.ds(4 * g, 4), b, side] = part_b.astype(low)
        return carry

    def grad_all(slot, put):
        def step(g, carry):
            grad(g, slot, ebuf.at[g, slot], dbuf.at[g, slot], lambda side, x: put(pl.ds(4 * g, 4), side, x))
            return carry

        lax.fori_loop(0, KVH, step, 0)


    group = head // 4
    nowhere = N * CAP

    def mark(d, carry):
        first, second = jnp.int32(N), jnp.int32(N)
        for p in range(N):
            entry = kept_blocks[group, d * N + p]
            inner = jnp.where((entry >> 4) == seq, entry & (N - 1), N)
            second = jnp.where(first < N, jnp.where(second < N, second, inner), second)
            first = jnp.where(first < N, first, inner)
        marks[CAP * d] = first
        marks[CAP * d + 1] = second
        return carry

    def places():
        owners = [kept_blocks[group, seq * N + p] >> 4 for p in range(N)]
        found = []
        for p in range(N):
            rank = jnp.int32(0)
            for r in range(p):
                rank = rank + jnp.where(owners[r] == owners[p], 1, 0)
            found.append(CAP * owners[p] + rank)
        return found

    def fill(i, carry):
        which = jnp.int32(N)
        for p in range(N):
            which = jnp.where(slot_of[p] == i, p, which)
        fills[i] = which
        return carry

    def link(i, carry):
        which, key = jnp.int32(nowhere), marks[i]
        for r in range(N * CAP):
            which = jnp.where((marks[r] == key) & (r < i), r, which)
        links[i] = which
        return carry

    def last(z, carry):
        which = jnp.int32(nowhere)
        for r in range(N * CAP):
            which = jnp.where(marks[r] == z, r, which)
        lasts[z] = which
        return carry


    first = exchange(own, rows_in, s1, r1, head, "head")

    def sink_send(k):
        return remote(own.at[k], piece, ss1.at[k], rs1.at[0], {"seq": k})

    @pl.when((seq == 0) & (head < SINK_MOST))
    def _():
        for k in range(1, N):
            sink_send(k).start()

    steps = []

    def relay(w):
        for c in range(CHUNKS):
            at = pl.ds(c * (N // CHUNKS), N // CHUNKS)
            i = w * CHUNKS + c
            src = own.at[at] if w == 0 else win.at[w - 1, at]
            if w > 0:
                steps[i - CHUNKS].wait_recv()
            steps.append(remote(src, win.at[w, at], sw.at[i], rw.at[i], after))
            steps[i].start()

    relay(0)
    rows_in[head] = own[head]

    @pl.when((seq == 0) & (head < SINK_MOST))
    def _():
        piece[...] = own[0]

    for copy in loads:
        copy.wait()
    for raw, buf in ((q_raw, qbuf), (g_raw, gbuf)):
        for pair in range(KVH // 2):
            x = raw[:, 16 * pair : 16 * (pair + 1), :].astype(wide)
            for m in range(2):
                buf[2 * pair + m] = x[:, 8 * m : 8 * (m + 1)].reshape(COLUMNS, HD).astype(low)
    mine = lax.rem(head, 4)

    def piece_far(k):
        return remote(piece, pieces.at[mine], ss2.at[k], rs2.at[mine], {"head": lax.rem(head + 4 * k, N)})

    def piece_near(k):
        to = lax.rem(head + k, N)
        return remote(pieces.at[mine], pieces.at[mine], ss2.at[k], rs2.at[mine], {"head": to})

    @pl.when((seq > 0) & (head < SINK_MOST))
    def _():
        remote(own.at[0], piece, ss1.at[0], rs1.at[0], {"seq": 0}).wait_recv()

    @pl.when(head < SINK_MOST)
    def _():
        for k in (2, 1, 3):
            piece_far(k).start()
        pieces[head] = piece[...]

    lax.fori_loop(0, N, mark, 0)
    score_all(SINK_MOST, own)

    for copy in first:
        copy.wait_recv()
    for k in range(N):
        for c in range(CAP):
            slots_out[k, c] = rows_in[jnp.minimum(marks[k * CAP + c], N - 1)]
    second = exchange(slots_out, slots_in, s2, r2, seq, "seq")
    slots_in[seq] = slots_out[seq]

    @pl.when((mine < SINK_MOST) & (head >= SINK_MOST))
    def _():
        remote(piece, pieces.at[mine], ss2.at[0], rs2.at[mine], {"head": mine}).wait_recv()

    @pl.when(mine < SINK_MOST)
    def _():
        for k in NEAR:
            piece_near(k).start()

    relay(1)
    score_all(SINK_MOST + 1, win.at[0])
    slot_of = places()

    for b in range(SINK_MOST):

        @pl.when(mine != b)
        def _():
            remote(piece, pieces.at[b], ss2.at[0], rs2.at[b], {"head": b}).wait_recv()

    spread = []
    for k in ORDER:
        to = lax.rem(seq + k, N)
        spread.append(remote(pieces, sink.at[seq], ss3.at[k], rs3.at[k], {"seq": to}))
        spread[-1].start()
    sink[seq] = pieces[...]

    for copy in second:
        copy.wait_recv()
    for k in range(N):
        far_out[k] = slots_in[slot_of[k] >> 1, slot_of[k] & 1]
    third = exchange(far_out, kept, s3, r3, head, "head")
    kept[head] = far_out[head]

    relay(2)
    score_all(SINK_MOST + 2, win.at[1])

    for copy in spread:
        copy.wait_recv()
    lax.fori_loop(0, KVH, score_sinks, 0)
    for copy in steps[2 * CHUNKS :]:
        copy.wait_recv()
    score_all(SINK_MOST + 3, win.at[2])
    for copy in third:
        copy.wait_recv()


    def kept_step(g, carry):
        score(g, SLOTS - 1, part(kept, g, 0), part(kept, g, 1), efar, dfar)
        combine(g)

        def put(side, x):
            tkept[pl.ds(4 * g, 4), side] = x.astype(low)

        grad(g, SLOTS - 1, efar, dfar, put)
        return carry

    lax.fori_loop(0, KVH, kept_step, 0, unroll=True)
    first_back = exchange(tkept, rows, t1, v1, head, "head")
    rows[head] = tkept[head]
    rows[N] = jnp.zeros(PIECE, low)

    lax.fori_loop(0, KVH, grad_sinks, 0)
    spread_back = exchange(tsink, sink_in, ts3, vs3, seq, "seq")
    sink_in[seq] = tsink[seq]

    def put_hop(at, side, x):
        hop_out[0, at, side] = x.astype(low)

    grad_all(SLOTS - 2, put_hop)
    hops = []

    def hop(w):
        for c in range(CHUNKS):
            at = pl.ds(c * (N // CHUNKS), N // CHUNKS)
            i = w * CHUNKS + c
            if w > 0:
                hops[i - CHUNKS].wait_recv()
                hop_out[w, at] = (near[WIN_MOST - 1 - w, at] + hop_in[w - 1, at].astype(wide)).astype(low)
            hops.append(remote(hop_out.at[w, at], hop_in.at[w, at], tw.at[i], vw.at[i], before))
            hops[i].start()

    hop(0)
    lax.fori_loop(0, N * CAP, fill, 0)

    def put_near(n):
        def put(at, side, x):
            near[n, at, side] = x

        return put

    grad_all(SINK_MOST + 2, put_near(2))

    for copy in first_back:
        copy.wait_recv()
    for k in range(N):
        for c in range(CAP):
            back_out[k, c] = rows[fills[k * CAP + c]]
    second_back = exchange(back_out, back_in, t2, v2, seq, "seq")
    back_in[seq] = back_out[seq]

    for copy in spread_back:
        copy.wait_recv()
    for b in range(SINK_MOST):
        term = sink_in[0, b].astype(wide)
        for k in range(1, N):
            term = term + sink_in[k, b].astype(wide)
        shares[b] = term.astype(low)

    def share_near(b):
        r = lax.rem(head + 4 - b, 4)
        to = lax.rem(jnp.where(r == 3, head + 1, head + N - r), N)
        return remote(shares.at[b], shares_in.at[r], ts2.at[b], vs2.at[r], {"head": to})

    for b in range(SINK_MOST):

        @pl.when(mine != b)
        def _():
            share_near(b).start()

    hop(1)
    grad_all(SINK_MOST + 1, put_near(1))

    def share_far():
        k = 3 + head // 4
        return remote(share, shares_far.at[k - 4], ts2.at[3], vs2.at[k], {"head": mine})

    @pl.when(mine < SINK_MOST)
    def _():
        term = shares[mine].astype(wide)
        for k in range(1, 4):
            remote(shares.at[0], shares_in.at[k], ts2.at[3], vs2.at[k], {"head": mine}).wait_recv()
            term = term + shares_in[k].astype(wide)
        share[...] = term

    @pl.when((mine < SINK_MOST) & (head >= SINK_MOST))
    def _():
        share_far().start()

    lax.fori_loop(0, N * CAP, link, 0)
    lax.fori_loop(0, N, last, 0)
    run[...] = jnp.zeros(run.shape, wide)

    for copy in second_back:
        copy.wait_recv()
    for k in range(N):
        for c in range(CAP):
            i = k * CAP + c
            run[i] = back_in[k, c].astype(wide) + run[links[i]]
    for k in range(N):
        sums[k] = run[lasts[k]].astype(low)
    third_back = exchange(sums, sums_in, t3, v3, head, "head")
    sums_in[head] = sums[head]

    hop(2)

    grad_all(SINK_MOST, put_near(0))

    for g in range(KVH):
        turned = lax.dot_general(kbuf[g], sbuf[g], TN, preferred_element_type=wide)
        m = g % 2
        dqbuf[:, GROUP * m : GROUP * (m + 1), :] = (turned.T * scale).reshape(BLK, GROUP, HD)
        if m == 1:
            dq[:, GROUP * (g - 1) : GROUP * (g + 1), :] = dqbuf[...].astype(low)

    def whole_send():
        return remote(whole_out, whole.at[seq], ts1.at[0], vs1.at[seq], {"seq": 0})

    @pl.when(head < SINK_MOST)
    def _():
        term = share[...]
        for k in range(4, 7):
            remote(share, shares_far.at[k - 4], ts2.at[3], vs2.at[k], {"head": mine}).wait_recv()
            term = term + shares_far[k - 4]
        whole_out[...] = term

    @pl.when((head < SINK_MOST) & (seq > 0))
    def _():
        whole_send().start()

    for copy in hops[2 * CHUNKS :]:
        copy.wait_recv()
    total[...] = near[0] + hop_in[2].astype(wide)
    for copy in third_back:
        copy.wait_recv()
    total[...] = total[...] + sums_in[...].astype(wide)

    @pl.when((head < SINK_MOST) & (seq == 0))
    def _():
        whole[0] = whole_out[...]
        for k in range(1, N):
            remote(whole_out, whole.at[k], ts1.at[0], vs1.at[k], {"seq": k}).wait_recv()
        total[...] = total[...] + whole[...]

    for side, ref in ((0, dk), (1, dv)):
        heads = [total[4 * g : 4 * (g + 1), side].reshape(BLK, HD) for g in range(KVH)]
        ref[...] = jnp.stack(heads, axis=1).astype(low)


    for copy in steps + first + second + third + spread:
        copy.wait_send()
    for copy in hops + first_back + second_back + third_back + spread_back:
        copy.wait_send()

    @pl.when((seq == 0) & (head < SINK_MOST))
    def _():
        for k in range(1, N):
            sink_send(k).wait_send()

    @pl.when(head < SINK_MOST)
    def _():
        for k in (2, 1, 3):
            piece_far(k).wait_send()

    @pl.when(mine < SINK_MOST)
    def _():
        for k in NEAR:
            piece_near(k).wait_send()

    for b in range(SINK_MOST):

        @pl.when(mine != b)
        def _():
            share_near(b).wait_send()

    @pl.when((mine < SINK_MOST) & (head >= SINK_MOST))
    def _():
        share_far().wait_send()

    @pl.when((head < SINK_MOST) & (seq > 0))
    def _():
        whole_send().wait_send()


def attend(kept_blocks, sink_blocks, window_blocks, q, g, keys, values):
    low, wide = jnp.bfloat16, jnp.float32
    vmem = pl.BlockSpec(memory_space=pltpu.VMEM)
    smem = pl.BlockSpec(memory_space=pltpu.SMEM)
    hbm = pl.BlockSpec(memory_space=pl.ANY)
    dma = pltpu.SemaphoreType.DMA

    def lows(*lead):
        return pltpu.VMEM(lead + PIECE, low)

    def wides(*lead):
        return pltpu.VMEM(lead + PIECE, wide)

    raw = pltpu.VMEM((BLK, KVH * GROUP, HD), low)
    flat = pltpu.VMEM((KVH, COLUMNS, HD), low)
    rows = pltpu.VMEM((KVH, SLOTS, COLUMNS), wide)
    return pl.pallas_call(
        kernel,
        out_shape=(
            jax.ShapeDtypeStruct((BLK, KVH * GROUP, HD), low),
            jax.ShapeDtypeStruct((BLK, KVH, HD), low),
            jax.ShapeDtypeStruct((BLK, KVH, HD), low),
        ),
        in_specs=[smem, smem, smem, hbm, hbm, vmem, vmem],
        out_specs=(vmem, vmem, vmem),
        scratch_shapes=[
            lows(N),
            lows(N), lows(N, CAP), lows(N, CAP), lows(N), lows(), lows(SINK_MOST),
            lows(N, SINK_MOST), lows(WIN_MOST - 1, N), lows(N),
            lows(N, SINK_MOST), lows(N), wides(WIN_MOST - 1, N), lows(N + 1), lows(N, CAP), lows(N, CAP),
            wides(N * CAP + 1), lows(N), lows(N),
            lows(N, SINK_MOST), lows(SINK_MOST), lows(4), wides(3), wides(), wides(), wides(N),
            lows(WIN_MOST - 1, N), lows(WIN_MOST - 1, N), wides(N),
            raw, raw, flat, flat,
            pltpu.VMEM((KVH, SLOTS * BLK, HD), low),
            pltpu.VMEM((KVH, SLOTS - 1, BLK, COLUMNS), wide),
            pltpu.VMEM((KVH, SLOTS - 1, BLK, COLUMNS), wide),
            pltpu.VMEM((KVH, SLOTS * BLK, COLUMNS), low),
            pltpu.VMEM((BLK, COLUMNS), wide),
            pltpu.VMEM((BLK, COLUMNS), wide),
            rows, rows, rows, rows,
            pltpu.VMEM((KVH, 1, COLUMNS), wide),
            pltpu.VMEM((BLK, 2 * GROUP, HD), wide),
            pltpu.SMEM((N * CAP,), jnp.int32), pltpu.SMEM((N * CAP,), jnp.int32),
            pltpu.SMEM((N * CAP,), jnp.int32), pltpu.SMEM((N,), jnp.int32),
            dma((2,)),
            dma((3 * CHUNKS,)), dma((3 * CHUNKS,)), dma((N,)), dma((N,)), dma((N,)), dma((N,)), dma((N,)), dma((N,)),
            dma((N,)), dma((1,)), dma((N,)), dma((N,)), dma((N,)), dma((N,)),
            dma((3 * CHUNKS,)), dma((3 * CHUNKS,)), dma((N,)), dma((N,)), dma((N,)), dma((N,)), dma((N,)), dma((N,)),
            dma((1,)), dma((N,)), dma((4,)), dma((8,)), dma((N,)), dma((N,)),
        ],
        compiler_params=pltpu.CompilerParams(
            collective_id=0, has_side_effects=True, vmem_limit_bytes=VMEM_LIMIT
        ),
        name="attend",
    )(kept_blocks, sink_blocks, window_blocks, q, g, keys, values)


def body(queries, keys, values, out_grad, kept_blocks, sink_blocks, window_blocks):
    lists = kept_blocks.reshape(KVH, N * N)
    return attend(lists, sink_blocks, window_blocks, queries, out_grad, keys, values)


def solution(mesh):
    tokens = P(("dp", "seq", "head"), None, None)
    return jax.shard_map(
        body,
        mesh=mesh,
        in_specs=(tokens, tokens, tokens, tokens, P(), P(), P()),
        out_specs=(tokens, tokens, tokens),
        check_vma=False,
    )
```

```python
import math

import jax
import jax.numpy as jnp
from jax import lax
from jax.experimental import pallas as pl
from jax.experimental.pallas import tpu as pltpu
from jax.sharding import PartitionSpec as P

BLK = 128
SINK_MOST = 3
WIN_MOST = 4
SLOTS = 8
N = 16
KVH = 4
GROUP = 8
HD = 128
CAP = 2
ROWS = 32
PIECE = (2, ROWS, HD)
MESH = pl.DeviceIdType.MESH
VMEM_LIMIT = 60 * 1024 * 1024


def remote(src, dst, send, recv, device):
    return pltpu.make_async_remote_copy(
        src_ref=src, dst_ref=dst, send_sem=send, recv_sem=recv, device_id=device, device_id_type=MESH
    )


def neighbours(seq, head):
    wrap_up = (head == N - 1).astype(jnp.int32)
    wrap_down = (head == 0).astype(jnp.int32)
    after = {"seq": lax.rem(seq + wrap_up, N), "head": lax.rem(head + 1, N)}
    before = {"seq": lax.rem(seq + N - wrap_down, N), "head": lax.rem(head + N - 1, N)}
    return before, after


def greet(seq, head, before, after):
    barrier = pltpu.get_barrier_semaphore()
    for k in range(1, N):
        pl.semaphore_signal(
            barrier, inc=1, device_id={"head": lax.rem(head + k, N)}, device_id_type=MESH
        )
        pl.semaphore_signal(
            barrier, inc=1, device_id={"seq": lax.rem(seq + k, N)}, device_id_type=MESH
        )
    pl.semaphore_signal(barrier, inc=1, device_id=before, device_id_type=MESH)
    pl.semaphore_signal(barrier, inc=1, device_id=after, device_id_type=MESH)
    pl.semaphore_wait(barrier, 2 * (N - 1) + 2)


ORDERS = {
    "head": [8] + [k for i in range(7, 0, -1) for k in (i, N - i)],
    "seq": [10, 6, 14, 9, 11, 2, 8, 5, 7, 13, 15, 1, 3, 4, 12],
}
COLS = 256
CHUNKS = 2
NEAR = (2, 1, N - 1)
COLUMNS = BLK * GROUP
LOWEST = -1e30
NT = (((1,), (1,)), ((), ()))
NN = (((1,), (0,)), ((), ()))
TN = (((0,), (0,)), ((), ()))


def exchange(src, dst, send, recv, me, axis):
    copies = []
    for k in ORDERS[axis]:
        to = lax.rem(me + k, N)
        copies.append(remote(src.at[to], dst.at[me], send.at[k], recv.at[k], {axis: to}))
        copies[-1].start()
    return copies


def kernel(
    kept_blocks, sink_blocks, window_blocks, q_hbm, g_hbm, keys, values, dq, dk, dv,
    own, rows_in, slots_out, slots_in, far_out, piece, pieces, sink, win, kept,
    tsink, tkept, near, rows, back_out, back_in, run, sums, sums_in,
    sink_in, shares, shares_in, shares_far, share, whole_out, whole, hop_out, hop_in, total,
    q_raw, g_raw, qbuf, gbuf, kbuf, ebuf, dbuf, sbuf, efar, dfar, tops, norms, deltas, factors, centre, dqbuf,
    marks, fills, links, lasts, load,
    sw, rw, s1, r1, s2, r2, s3, r3, ss1, rs1, ss2, rs2, ss3, rs3,
    tw, vw, t1, v1, t2, v2, t3, v3, ts1, vs1, ts2, vs2, ts3, vs3,
):
    seq, head = lax.axis_index("seq"), lax.axis_index("head")
    low, wide = jnp.bfloat16, jnp.float32
    scale = 1.0 / math.sqrt(HD)
    before, after = neighbours(seq, head)
    loads = [
        pltpu.make_async_copy(q_hbm, q_raw, load.at[0]),
        pltpu.make_async_copy(g_hbm, g_raw, load.at[1]),
    ]
    for copy in loads:
        copy.start()
    for side, ref in ((0, keys), (1, values)):
        x = ref[...].astype(wide)
        for g in range(KVH):
            own[4 * g : 4 * (g + 1), side] = x[:, g, :].astype(low).reshape(4, ROWS, HD)
    greet(seq, head, before, after)


    current = seq * N + head

    def allowed(g, slot):
        sinks, windows = sink_blocks[g], window_blocks[g]
        if slot < SINK_MOST:
            return (slot < sinks) & (slot <= current) & (current - slot >= windows)
        if slot < SLOTS - 1:
            return (slot - SINK_MOST < windows) & (slot - SINK_MOST <= current)
        named = kept_blocks[g, current]
        return (named <= current) & (named >= sinks) & (current - named >= windows)

    def part(ref, g, side):
        return ref[pl.ds(4 * g, 4), side].reshape(BLK, HD)

    def score(g, slot, k, v, e_ref, d_ref):
        kbuf[g, slot * BLK : (slot + 1) * BLK, :] = k
        bias = jnp.where(allowed(g, slot), 0.0, -jnp.inf)
        for i in range(COLUMNS // COLS):
            here = slice(i * COLS, (i + 1) * COLS)
            s = lax.dot_general(k, qbuf[g, here, :], NT, preferred_element_type=wide) * scale
            if slot == SINK_MOST:
                u = lax.broadcasted_iota(jnp.int32, (BLK, COLS), 0)
                t = (lax.broadcasted_iota(jnp.int32, (BLK, COLS), 1) + i * COLS) // GROUP
                s = jnp.where(u <= t, s, -jnp.inf)
            else:
                s = s + bias
            top = jnp.maximum(jnp.max(s, axis=0, keepdims=True), LOWEST)
            e = jnp.exp(s - top)
            d = lax.dot_general(v, gbuf[g, here, :], NT, preferred_element_type=wide)
            e_ref[:, here] = e
            d_ref[:, here] = d
            tops[g, slot : slot + 1, here] = top
            norms[g, slot : slot + 1, here] = jnp.sum(e, axis=0, keepdims=True)
            deltas[g, slot : slot + 1, here] = jnp.sum(e * d, axis=0, keepdims=True)

    def score_all(slot, ref):
        def step(g, carry):
            score(g, slot, part(ref, g, 0), part(ref, g, 1), ebuf.at[g, slot], dbuf.at[g, slot])
            return carry

        lax.fori_loop(0, KVH, step, 0)

    def score_sinks(g, carry):
        k = jnp.concatenate([sink[pl.ds(4 * g, 4), b, 0].reshape(BLK, HD) for b in range(SINK_MOST)])
        v = jnp.concatenate([sink[pl.ds(4 * g, 4), b, 1].reshape(BLK, HD) for b in range(SINK_MOST)])
        kbuf[g, : SINK_MOST * BLK, :] = k
        biases = [jnp.where(allowed(g, b), 0.0, -jnp.inf) for b in range(SINK_MOST)]
        for i in range(COLUMNS // COLS):
            here = slice(i * COLS, (i + 1) * COLS)
            s = lax.dot_general(k, qbuf[g, here, :], NT, preferred_element_type=wide) * scale
            d = lax.dot_general(v, gbuf[g, here, :], NT, preferred_element_type=wide)
            for b in range(SINK_MOST):
                rows_b = slice(b * BLK, (b + 1) * BLK)
                t = s[rows_b] + biases[b]
                top = jnp.maximum(jnp.max(t, axis=0, keepdims=True), LOWEST)
                e = jnp.exp(t - top)
                ebuf[g, b, :, here] = e
                dbuf[g, b, :, here] = d[rows_b]
                tops[g, b : b + 1, here] = top
                norms[g, b : b + 1, here] = jnp.sum(e, axis=0, keepdims=True)
                deltas[g, b : b + 1, here] = jnp.sum(e * d[rows_b], axis=0, keepdims=True)
        return carry

    def combine(g):
        t = tops[g]
        w = jnp.exp(t - jnp.max(t, axis=0, keepdims=True))
        inverse = 1.0 / jnp.sum(w * norms[g], axis=0, keepdims=True)
        factors[g] = w * inverse
        centre[g] = jnp.sum(w * deltas[g], axis=0, keepdims=True) * inverse

    def grad(g, slot, e_ref, d_ref, put):
        p = e_ref[...] * factors[g, slot : slot + 1, :]
        ds = (p * (d_ref[...] - centre[g])).astype(low)
        sbuf[g, slot * BLK : (slot + 1) * BLK, :] = ds
        put(0, (lax.dot_general(ds, qbuf[g], NN, preferred_element_type=wide) * scale).reshape(4, ROWS, HD))
        dv = lax.dot_general(p.astype(low), gbuf[g], NN, preferred_element_type=wide)
        put(1, dv.reshape(4, ROWS, HD))

    def grad_sinks(g, carry):
        terms = []
        for b in range(SINK_MOST):
            p = ebuf[g, b] * factors[g, b : b + 1, :]
            terms.append((p.astype(low), (p * (dbuf[g, b] - centre[g])).astype(low)))
        p = jnp.concatenate([t[0] for t in terms])
        ds = jnp.concatenate([t[1] for t in terms])
        sbuf[g, : SINK_MOST * BLK, :] = ds
        dk = lax.dot_general(ds, qbuf[g], NN, preferred_element_type=wide) * scale
        dv = lax.dot_general(p, gbuf[g], NN, preferred_element_type=wide)
        for b in range(SINK_MOST):
            for side, x in ((0, dk), (1, dv)):
                part_b = x[b * BLK : (b + 1) * BLK].reshape(4, ROWS, HD)
                tsink[pl.ds(4 * g, 4), b, side] = part_b.astype(low)
        return carry

    def grad_all(slot, put):
        def step(g, carry):
            grad(g, slot, ebuf.at[g, slot], dbuf.at[g, slot], lambda side, x: put(pl.ds(4 * g, 4), side, x))
            return carry

        lax.fori_loop(0, KVH, step, 0)


    group = head // 4
    nowhere = N * CAP

    def mark(d, carry):
        first, second = jnp.int32(N), jnp.int32(N)
        for p in range(N):
            entry = kept_blocks[group, d * N + p]
            inner = jnp.where((entry >> 4) == seq, entry & (N - 1), N)
            second = jnp.where(first < N, jnp.where(second < N, second, inner), second)
            first = jnp.where(first < N, first, inner)
        marks[CAP * d] = first
        marks[CAP * d + 1] = second
        return carry

    def places():
        owners = [kept_blocks[group, seq * N + p] >> 4 for p in range(N)]
        found = []
        for p in range(N):
            rank = jnp.int32(0)
            for r in range(p):
                rank = rank + jnp.where(owners[r] == owners[p], 1, 0)
            found.append(CAP * owners[p] + rank)
        return found

    def fill(i, carry):
        which = jnp.int32(N)
        for p in range(N):
            which = jnp.where(slot_of[p] == i, p, which)
        fills[i] = which
        return carry

    def link(i, carry):
        which, key = jnp.int32(nowhere), marks[i]
        for r in range(N * CAP):
            which = jnp.where((marks[r] == key) & (r < i), r, which)
        links[i] = which
        return carry

    def last(z, carry):
        which = jnp.int32(nowhere)
        for r in range(N * CAP):
            which = jnp.where(marks[r] == z, r, which)
        lasts[z] = which
        return carry


    first = exchange(own, rows_in, s1, r1, head, "head")

    def sink_send(k):
        return remote(own.at[k], piece, ss1.at[k], rs1.at[0], {"seq": k})

    @pl.when((seq == 0) & (head < SINK_MOST))
    def _():
        for k in range(1, N):
            sink_send(k).start()

    steps = []

    def relay(w):
        for c in range(CHUNKS):
            at = pl.ds(c * (N // CHUNKS), N // CHUNKS)
            i = w * CHUNKS + c
            src = own.at[at] if w == 0 else win.at[w - 1, at]
            if w > 0:
                steps[i - CHUNKS].wait_recv()
            steps.append(remote(src, win.at[w, at], sw.at[i], rw.at[i], after))
            steps[i].start()

    relay(0)
    rows_in[head] = own[head]

    @pl.when((seq == 0) & (head < SINK_MOST))
    def _():
        piece[...] = own[0]

    for copy in loads:
        copy.wait()
    for raw, buf in ((q_raw, qbuf), (g_raw, gbuf)):
        for pair in range(KVH // 2):
            x = raw[:, 16 * pair : 16 * (pair + 1), :].astype(wide)
            for m in range(2):
                buf[2 * pair + m] = x[:, 8 * m : 8 * (m + 1)].reshape(COLUMNS, HD).astype(low)
    mine = lax.rem(head, 4)

    def piece_far(k):
        return remote(piece, pieces.at[mine], ss2.at[k], rs2.at[mine], {"head": lax.rem(head + 4 * k, N)})

    def piece_near(k):
        to = lax.rem(head + k, N)
        return remote(pieces.at[mine], pieces.at[mine], ss2.at[k], rs2.at[mine], {"head": to})

    @pl.when((seq > 0) & (head < SINK_MOST))
    def _():
        remote(own.at[0], piece, ss1.at[0], rs1.at[0], {"seq": 0}).wait_recv()

    @pl.when(head < SINK_MOST)
    def _():
        for k in (2, 1, 3):
            piece_far(k).start()
        pieces[head] = piece[...]

    lax.fori_loop(0, N, mark, 0)
    score_all(SINK_MOST, own)

    for copy in first:
        copy.wait_recv()
    for k in range(N):
        for c in range(CAP):
            slots_out[k, c] = rows_in[jnp.minimum(marks[k * CAP + c], N - 1)]
    second = exchange(slots_out, slots_in, s2, r2, seq, "seq")
    slots_in[seq] = slots_out[seq]

    @pl.when((mine < SINK_MOST) & (head >= SINK_MOST))
    def _():
        remote(piece, pieces.at[mine], ss2.at[0], rs2.at[mine], {"head": mine}).wait_recv()

    @pl.when(mine < SINK_MOST)
    def _():
        for k in NEAR:
            piece_near(k).start()

    relay(1)
    score_all(SINK_MOST + 1, win.at[0])
    slot_of = places()

    for b in range(SINK_MOST):

        @pl.when(mine != b)
        def _():
            remote(piece, pieces.at[b], ss2.at[0], rs2.at[b], {"head": b}).wait_recv()

    spread = []
    for k in ORDERS["seq"]:
        to = lax.rem(seq + k, N)
        spread.append(remote(pieces, sink.at[seq], ss3.at[k], rs3.at[k], {"seq": to}))
        spread[-1].start()
    sink[seq] = pieces[...]

    for copy in second:
        copy.wait_recv()
    for k in range(N):
        far_out[k] = slots_in[slot_of[k] >> 1, slot_of[k] & 1]
    third = exchange(far_out, kept, s3, r3, head, "head")
    kept[head] = far_out[head]

    relay(2)
    score_all(SINK_MOST + 2, win.at[1])

    for copy in spread:
        copy.wait_recv()
    lax.fori_loop(0, KVH, score_sinks, 0)
    for copy in steps[2 * CHUNKS :]:
        copy.wait_recv()
    score_all(SINK_MOST + 3, win.at[2])
    for copy in third:
        copy.wait_recv()


    def kept_step(g, carry):
        score(g, SLOTS - 1, part(kept, g, 0), part(kept, g, 1), efar, dfar)
        combine(g)

        def put(side, x):
            tkept[pl.ds(4 * g, 4), side] = x.astype(low)

        grad(g, SLOTS - 1, efar, dfar, put)
        return carry

    lax.fori_loop(0, KVH, kept_step, 0, unroll=True)
    first_back = exchange(tkept, rows, t1, v1, head, "head")
    rows[head] = tkept[head]
    rows[N] = jnp.zeros(PIECE, low)

    lax.fori_loop(0, KVH, grad_sinks, 0)
    spread_back = exchange(tsink, sink_in, ts3, vs3, seq, "seq")
    sink_in[seq] = tsink[seq]

    def put_hop(at, side, x):
        hop_out[0, at, side] = x.astype(low)

    grad_all(SLOTS - 2, put_hop)
    hops = []

    def hop(w):
        for c in range(CHUNKS):
            at = pl.ds(c * (N // CHUNKS), N // CHUNKS)
            i = w * CHUNKS + c
            if w > 0:
                hops[i - CHUNKS].wait_recv()
                hop_out[w, at] = (near[WIN_MOST - 1 - w, at] + hop_in[w - 1, at].astype(wide)).astype(low)
            hops.append(remote(hop_out.at[w, at], hop_in.at[w, at], tw.at[i], vw.at[i], before))
            hops[i].start()

    hop(0)
    lax.fori_loop(0, N * CAP, fill, 0)

    def put_near(n):
        def put(at, side, x):
            near[n, at, side] = x

        return put

    grad_all(SINK_MOST + 2, put_near(2))

    for copy in first_back:
        copy.wait_recv()
    for k in range(N):
        for c in range(CAP):
            back_out[k, c] = rows[fills[k * CAP + c]]
    second_back = exchange(back_out, back_in, t2, v2, seq, "seq")
    back_in[seq] = back_out[seq]

    for copy in spread_back:
        copy.wait_recv()
    for b in range(SINK_MOST):
        term = sink_in[0, b].astype(wide)
        for k in range(1, N):
            term = term + sink_in[k, b].astype(wide)
        shares[b] = term.astype(low)

    def share_near(b):
        r = lax.rem(head + 4 - b, 4)
        to = lax.rem(jnp.where(r == 3, head + 1, head + N - r), N)
        return remote(shares.at[b], shares_in.at[r], ts2.at[b], vs2.at[r], {"head": to})

    for b in range(SINK_MOST):

        @pl.when(mine != b)
        def _():
            share_near(b).start()

    hop(1)
    grad_all(SINK_MOST + 1, put_near(1))

    def share_far():
        k = 3 + head // 4
        return remote(share, shares_far.at[k - 4], ts2.at[3], vs2.at[k], {"head": mine})

    @pl.when(mine < SINK_MOST)
    def _():
        term = shares[mine].astype(wide)
        for k in range(1, 4):
            remote(shares.at[0], shares_in.at[k], ts2.at[3], vs2.at[k], {"head": mine}).wait_recv()
            term = term + shares_in[k].astype(wide)
        share[...] = term

    @pl.when((mine < SINK_MOST) & (head >= SINK_MOST))
    def _():
        share_far().start()

    lax.fori_loop(0, N * CAP, link, 0)
    lax.fori_loop(0, N, last, 0)
    run[...] = jnp.zeros(run.shape, wide)

    for copy in second_back:
        copy.wait_recv()
    for k in range(N):
        for c in range(CAP):
            i = k * CAP + c
            run[i] = back_in[k, c].astype(wide) + run[links[i]]
    for k in range(N):
        sums[k] = run[lasts[k]].astype(low)
    third_back = exchange(sums, sums_in, t3, v3, head, "head")
    sums_in[head] = sums[head]

    hop(2)

    grad_all(SINK_MOST, put_near(0))

    for g in range(KVH):
        turned = lax.dot_general(kbuf[g], sbuf[g], TN, preferred_element_type=wide)
        m = g % 2
        dqbuf[:, GROUP * m : GROUP * (m + 1), :] = (turned.T * scale).reshape(BLK, GROUP, HD)
        if m == 1:
            dq[:, GROUP * (g - 1) : GROUP * (g + 1), :] = dqbuf[...].astype(low)

    def whole_send():
        return remote(whole_out, whole.at[seq], ts1.at[0], vs1.at[seq], {"seq": 0})

    @pl.when(head < SINK_MOST)
    def _():
        term = share[...]
        for k in range(4, 7):
            remote(share, shares_far.at[k - 4], ts2.at[3], vs2.at[k], {"head": mine}).wait_recv()
            term = term + shares_far[k - 4]
        whole_out[...] = term

    @pl.when((head < SINK_MOST) & (seq > 0))
    def _():
        whole_send().start()

    for copy in hops[2 * CHUNKS :]:
        copy.wait_recv()
    total[...] = near[0] + hop_in[2].astype(wide)
    for copy in third_back:
        copy.wait_recv()
    total[...] = total[...] + sums_in[...].astype(wide)

    @pl.when((head < SINK_MOST) & (seq == 0))
    def _():
        whole[0] = whole_out[...]
        for k in range(1, N):
            remote(whole_out, whole.at[k], ts1.at[0], vs1.at[k], {"seq": k}).wait_recv()
        total[...] = total[...] + whole[...]

    for side, ref in ((0, dk), (1, dv)):
        heads = [total[4 * g : 4 * (g + 1), side].reshape(BLK, HD) for g in range(KVH)]
        ref[...] = jnp.stack(heads, axis=1).astype(low)


    for copy in steps + first + second + third + spread:
        copy.wait_send()
    for copy in hops + first_back + second_back + third_back + spread_back:
        copy.wait_send()

    @pl.when((seq == 0) & (head < SINK_MOST))
    def _():
        for k in range(1, N):
            sink_send(k).wait_send()

    @pl.when(head < SINK_MOST)
    def _():
        for k in (2, 1, 3):
            piece_far(k).wait_send()

    @pl.when(mine < SINK_MOST)
    def _():
        for k in NEAR:
            piece_near(k).wait_send()

    for b in range(SINK_MOST):

        @pl.when(mine != b)
        def _():
            share_near(b).wait_send()

    @pl.when((mine < SINK_MOST) & (head >= SINK_MOST))
    def _():
        share_far().wait_send()

    @pl.when((head < SINK_MOST) & (seq > 0))
    def _():
        whole_send().wait_send()


def attend(kept_blocks, sink_blocks, window_blocks, q, g, keys, values):
    low, wide = jnp.bfloat16, jnp.float32
    vmem = pl.BlockSpec(memory_space=pltpu.VMEM)
    smem = pl.BlockSpec(memory_space=pltpu.SMEM)
    hbm = pl.BlockSpec(memory_space=pl.ANY)
    dma = pltpu.SemaphoreType.DMA

    def lows(*lead):
        return pltpu.VMEM(lead + PIECE, low)

    def wides(*lead):
        return pltpu.VMEM(lead + PIECE, wide)

    raw = pltpu.VMEM((BLK, KVH * GROUP, HD), low)
    flat = pltpu.VMEM((KVH, COLUMNS, HD), low)
    rows = pltpu.VMEM((KVH, SLOTS, COLUMNS), wide)
    return pl.pallas_call(
        kernel,
        out_shape=(
            jax.ShapeDtypeStruct((BLK, KVH * GROUP, HD), low),
            jax.ShapeDtypeStruct((BLK, KVH, HD), low),
            jax.ShapeDtypeStruct((BLK, KVH, HD), low),
        ),
        in_specs=[smem, smem, smem, hbm, hbm, vmem, vmem],
        out_specs=(vmem, vmem, vmem),
        scratch_shapes=[
            lows(N),
            lows(N), lows(N, CAP), lows(N, CAP), lows(N), lows(), lows(SINK_MOST),
            lows(N, SINK_MOST), lows(WIN_MOST - 1, N), lows(N),
            lows(N, SINK_MOST), lows(N), wides(WIN_MOST - 1, N), lows(N + 1), lows(N, CAP), lows(N, CAP),
            wides(N * CAP + 1), lows(N), lows(N),
            lows(N, SINK_MOST), lows(SINK_MOST), lows(4), wides(3), wides(), wides(), wides(N),
            lows(WIN_MOST - 1, N), lows(WIN_MOST - 1, N), wides(N),
            raw, raw, flat, flat,
            pltpu.VMEM((KVH, SLOTS * BLK, HD), low),
            pltpu.VMEM((KVH, SLOTS - 1, BLK, COLUMNS), wide),
            pltpu.VMEM((KVH, SLOTS - 1, BLK, COLUMNS), wide),
            pltpu.VMEM((KVH, SLOTS * BLK, COLUMNS), low),
            pltpu.VMEM((BLK, COLUMNS), wide),
            pltpu.VMEM((BLK, COLUMNS), wide),
            rows, rows, rows, rows,
            pltpu.VMEM((KVH, 1, COLUMNS), wide),
            pltpu.VMEM((BLK, 2 * GROUP, HD), wide),
            pltpu.SMEM((N * CAP,), jnp.int32), pltpu.SMEM((N * CAP,), jnp.int32),
            pltpu.SMEM((N * CAP,), jnp.int32), pltpu.SMEM((N,), jnp.int32),
            dma((2,)),
            dma((3 * CHUNKS,)), dma((3 * CHUNKS,)), dma((N,)), dma((N,)), dma((N,)), dma((N,)), dma((N,)), dma((N,)),
            dma((N,)), dma((1,)), dma((N,)), dma((N,)), dma((N,)), dma((N,)),
            dma((3 * CHUNKS,)), dma((3 * CHUNKS,)), dma((N,)), dma((N,)), dma((N,)), dma((N,)), dma((N,)), dma((N,)),
            dma((1,)), dma((N,)), dma((4,)), dma((8,)), dma((N,)), dma((N,)),
        ],
        compiler_params=pltpu.CompilerParams(
            collective_id=0, has_side_effects=True, vmem_limit_bytes=VMEM_LIMIT
        ),
        name="attend",
    )(kept_blocks, sink_blocks, window_blocks, q, g, keys, values)


def body(queries, keys, values, out_grad, kept_blocks, sink_blocks, window_blocks):
    lists = kept_blocks.reshape(KVH, N * N)
    return attend(lists, sink_blocks, window_blocks, queries, out_grad, keys, values)


def solution(mesh):
    tokens = P(("dp", "seq", "head"), None, None)
    return jax.shard_map(
        body,
        mesh=mesh,
        in_specs=(tokens, tokens, tokens, tokens, P(), P(), P()),
        out_specs=(tokens, tokens, tokens),
        check_vma=False,
    )
```

```python
import math

import jax
import jax.numpy as jnp
from jax import lax
from jax.experimental import pallas as pl
from jax.experimental.pallas import tpu as pltpu
from jax.sharding import PartitionSpec as P

BLK = 128
SINK_MOST = 3
WIN_MOST = 4
SLOTS = 8
N = 16
KVH = 4
GROUP = 8
HD = 128
CAP = 2
ROWS = 32
PIECE = (2, ROWS, HD)
MESH = pl.DeviceIdType.MESH
VMEM_LIMIT = 60 * 1024 * 1024


def remote(src, dst, send, recv, device):
    return pltpu.make_async_remote_copy(
        src_ref=src, dst_ref=dst, send_sem=send, recv_sem=recv, device_id=device, device_id_type=MESH
    )


def neighbours(seq, head):
    wrap_up = (head == N - 1).astype(jnp.int32)
    wrap_down = (head == 0).astype(jnp.int32)
    after = {"seq": lax.rem(seq + wrap_up, N), "head": lax.rem(head + 1, N)}
    before = {"seq": lax.rem(seq + N - wrap_down, N), "head": lax.rem(head + N - 1, N)}
    return before, after


def greet(seq, head, before, after):
    barrier = pltpu.get_barrier_semaphore()
    for k in range(1, N):
        pl.semaphore_signal(
            barrier, inc=1, device_id={"head": lax.rem(head + k, N)}, device_id_type=MESH
        )
        pl.semaphore_signal(
            barrier, inc=1, device_id={"seq": lax.rem(seq + k, N)}, device_id_type=MESH
        )
    pl.semaphore_signal(barrier, inc=1, device_id=before, device_id_type=MESH)
    pl.semaphore_signal(barrier, inc=1, device_id=after, device_id_type=MESH)
    pl.semaphore_wait(barrier, 2 * (N - 1) + 2)


ORDER = [8] + [k for i in range(1, 8) for k in (i, N - i)]
COLS = 256
CHUNKS = 2
NEAR = (2, 1, N - 1)
COLUMNS = BLK * GROUP
LOWEST = -1e30
NT = (((1,), (1,)), ((), ()))
NN = (((1,), (0,)), ((), ()))
TN = (((0,), (0,)), ((), ()))


def exchange(src, dst, send, recv, me, axis):
    copies = []
    for k in ORDER:
        to = lax.rem(me + k, N)
        copies.append(remote(src.at[to], dst.at[me], send.at[k], recv.at[k], {axis: to}))
        copies[-1].start()
    return copies


def kernel(
    kept_blocks, sink_blocks, window_blocks, q_hbm, g_hbm, keys, values, dq, dk, dv,
    own, rows_in, slots_out, slots_in, far_out, piece, pieces, sink, win, kept,
    tsink, tkept, near, rows, back_out, back_in, run, sums, sums_in,
    sink_in, shares, shares_in, shares_far, share, whole_out, whole, hop_out, hop_in, total,
    q_raw, g_raw, qbuf, gbuf, kbuf, ebuf, dbuf, sbuf, efar, dfar, tops, norms, deltas, factors, centre, dqbuf,
    marks, fills, links, lasts, load,
    sw, rw, s1, r1, s2, r2, s3, r3, ss1, rs1, ss2, rs2, ss3, rs3,
    tw, vw, t1, v1, t2, v2, t3, v3, ts1, vs1, ts2, vs2, ts3, vs3,
):
    seq, head = lax.axis_index("seq"), lax.axis_index("head")
    low, wide = jnp.bfloat16, jnp.float32
    scale = 1.0 / math.sqrt(HD)
    before, after = neighbours(seq, head)
    loads = [
        pltpu.make_async_copy(q_hbm, q_raw, load.at[0]),
        pltpu.make_async_copy(g_hbm, g_raw, load.at[1]),
    ]
    for copy in loads:
        copy.start()
    for side, ref in ((0, keys), (1, values)):
        x = ref[...].astype(wide)
        for g in range(KVH):
            own[4 * g : 4 * (g + 1), side] = x[:, g, :].astype(low).reshape(4, ROWS, HD)
    greet(seq, head, before, after)


    current = seq * N + head

    def allowed(g, slot):
        sinks, windows = sink_blocks[g], window_blocks[g]
        if slot < SINK_MOST:
            return (slot < sinks) & (slot <= current) & (current - slot >= windows)
        if slot < SLOTS - 1:
            return (slot - SINK_MOST < windows) & (slot - SINK_MOST <= current)
        named = kept_blocks[g, current]
        return (named <= current) & (named >= sinks) & (current - named >= windows)

    def part(ref, g, side):
        return ref[pl.ds(4 * g, 4), side].reshape(BLK, HD)

    def score(g, slot, k, v, e_ref, d_ref):
        kbuf[g, slot * BLK : (slot + 1) * BLK, :] = k
        bias = jnp.where(allowed(g, slot), 0.0, -jnp.inf)
        for i in range(COLUMNS // COLS):
            here = slice(i * COLS, (i + 1) * COLS)
            s = lax.dot_general(k, qbuf[g, here, :], NT, preferred_element_type=wide) * scale
            if slot == SINK_MOST:
                u = lax.broadcasted_iota(jnp.int32, (BLK, COLS), 0)
                t = (lax.broadcasted_iota(jnp.int32, (BLK, COLS), 1) + i * COLS) // GROUP
                s = jnp.where(u <= t, s, -jnp.inf)
            else:
                s = s + bias
            top = jnp.maximum(jnp.max(s, axis=0, keepdims=True), LOWEST)
            e = jnp.exp(s - top)
            d = lax.dot_general(v, gbuf[g, here, :], NT, preferred_element_type=wide)
            e_ref[:, here] = e
            d_ref[:, here] = d
            tops[g, slot : slot + 1, here] = top
            norms[g, slot : slot + 1, here] = jnp.sum(e, axis=0, keepdims=True)
            deltas[g, slot : slot + 1, here] = jnp.sum(e * d, axis=0, keepdims=True)

    def score_all(slot, ref):
        def step(g, carry):
            score(g, slot, part(ref, g, 0), part(ref, g, 1), ebuf.at[g, slot], dbuf.at[g, slot])
            return carry

        lax.fori_loop(0, KVH, step, 0, unroll=2)

    def score_sinks(g, carry):
        k = jnp.concatenate([sink[pl.ds(4 * g, 4), b, 0].reshape(BLK, HD) for b in range(SINK_MOST)])
        v = jnp.concatenate([sink[pl.ds(4 * g, 4), b, 1].reshape(BLK, HD) for b in range(SINK_MOST)])
        kbuf[g, : SINK_MOST * BLK, :] = k
        biases = [jnp.where(allowed(g, b), 0.0, -jnp.inf) for b in range(SINK_MOST)]
        for i in range(COLUMNS // COLS):
            here = slice(i * COLS, (i + 1) * COLS)
            s = lax.dot_general(k, qbuf[g, here, :], NT, preferred_element_type=wide) * scale
            d = lax.dot_general(v, gbuf[g, here, :], NT, preferred_element_type=wide)
            for b in range(SINK_MOST):
                rows_b = slice(b * BLK, (b + 1) * BLK)
                t = s[rows_b] + biases[b]
                top = jnp.maximum(jnp.max(t, axis=0, keepdims=True), LOWEST)
                e = jnp.exp(t - top)
                ebuf[g, b, :, here] = e
                dbuf[g, b, :, here] = d[rows_b]
                tops[g, b : b + 1, here] = top
                norms[g, b : b + 1, here] = jnp.sum(e, axis=0, keepdims=True)
                deltas[g, b : b + 1, here] = jnp.sum(e * d[rows_b], axis=0, keepdims=True)
        return carry

    def combine(g):
        t = tops[g]
        w = jnp.exp(t - jnp.max(t, axis=0, keepdims=True))
        inverse = 1.0 / jnp.sum(w * norms[g], axis=0, keepdims=True)
        factors[g] = w * inverse
        centre[g] = jnp.sum(w * deltas[g], axis=0, keepdims=True) * inverse

    def grad(g, slot, e_ref, d_ref, put):
        p = e_ref[...] * factors[g, slot : slot + 1, :]
        ds = (p * (d_ref[...] - centre[g])).astype(low)
        sbuf[g, slot * BLK : (slot + 1) * BLK, :] = ds
        put(0, (lax.dot_general(ds, qbuf[g], NN, preferred_element_type=wide) * scale).reshape(4, ROWS, HD))
        dv = lax.dot_general(p.astype(low), gbuf[g], NN, preferred_element_type=wide)
        put(1, dv.reshape(4, ROWS, HD))

    def grad_sinks(g, carry):
        terms = []
        for b in range(SINK_MOST):
            p = ebuf[g, b] * factors[g, b : b + 1, :]
            terms.append((p.astype(low), (p * (dbuf[g, b] - centre[g])).astype(low)))
        p = jnp.concatenate([t[0] for t in terms])
        ds = jnp.concatenate([t[1] for t in terms])
        sbuf[g, : SINK_MOST * BLK, :] = ds
        dk = lax.dot_general(ds, qbuf[g], NN, preferred_element_type=wide) * scale
        dv = lax.dot_general(p, gbuf[g], NN, preferred_element_type=wide)
        for b in range(SINK_MOST):
            for side, x in ((0, dk), (1, dv)):
                part_b = x[b * BLK : (b + 1) * BLK].reshape(4, ROWS, HD)
                tsink[pl.ds(4 * g, 4), b, side] = part_b.astype(low)
        return carry

    def grad_all(slot, put):
        def step(g, carry):
            grad(g, slot, ebuf.at[g, slot], dbuf.at[g, slot], lambda side, x: put(pl.ds(4 * g, 4), side, x))
            return carry

        lax.fori_loop(0, KVH, step, 0, unroll=2)


    group = head // 4
    nowhere = N * CAP

    def mark(d, carry):
        first, second = jnp.int32(N), jnp.int32(N)
        for p in range(N):
            entry = kept_blocks[group, d * N + p]
            inner = jnp.where((entry >> 4) == seq, entry & (N - 1), N)
            second = jnp.where(first < N, jnp.where(second < N, second, inner), second)
            first = jnp.where(first < N, first, inner)
        marks[CAP * d] = first
        marks[CAP * d + 1] = second
        return carry

    def places():
        owners = [kept_blocks[group, seq * N + p] >> 4 for p in range(N)]
        found = []
        for p in range(N):
            rank = jnp.int32(0)
            for r in range(p):
                rank = rank + jnp.where(owners[r] == owners[p], 1, 0)
            found.append(CAP * owners[p] + rank)
        return found

    def fill(i, carry):
        which = jnp.int32(N)
        for p in range(N):
            which = jnp.where(slot_of[p] == i, p, which)
        fills[i] = which
        return carry

    def link(i, carry):
        which, key = jnp.int32(nowhere), marks[i]
        for r in range(N * CAP):
            which = jnp.where((marks[r] == key) & (r < i), r, which)
        links[i] = which
        return carry

    def last(z, carry):
        which = jnp.int32(nowhere)
        for r in range(N * CAP):
            which = jnp.where(marks[r] == z, r, which)
        lasts[z] = which
        return carry


    first = exchange(own, rows_in, s1, r1, head, "head")

    def sink_send(k):
        return remote(own.at[k], piece, ss1.at[k], rs1.at[0], {"seq": k})

    @pl.when((seq == 0) & (head < SINK_MOST))
    def _():
        for k in range(1, N):
            sink_send(k).start()

    steps = []

    def relay(w):
        for c in range(CHUNKS):
            at = pl.ds(c * (N // CHUNKS), N // CHUNKS)
            i = w * CHUNKS + c
            src = own.at[at] if w == 0 else win.at[w - 1, at]
            if w > 0:
                steps[i - CHUNKS].wait_recv()
            steps.append(remote(src, win.at[w, at], sw.at[i], rw.at[i], after))
            steps[i].start()

    relay(0)
    rows_in[head] = own[head]

    @pl.when((seq == 0) & (head < SINK_MOST))
    def _():
        piece[...] = own[0]

    for copy in loads:
        copy.wait()
    for raw, buf in ((q_raw, qbuf), (g_raw, gbuf)):
        for pair in range(KVH // 2):
            x = raw[:, 16 * pair : 16 * (pair + 1), :].astype(wide)
            for m in range(2):
                buf[2 * pair + m] = x[:, 8 * m : 8 * (m + 1)].reshape(COLUMNS, HD).astype(low)
    mine = lax.rem(head, 4)

    def piece_far(k):
        return remote(piece, pieces.at[mine], ss2.at[k], rs2.at[mine], {"head": lax.rem(head + 4 * k, N)})

    def piece_near(k):
        to = lax.rem(head + k, N)
        return remote(pieces.at[mine], pieces.at[mine], ss2.at[k], rs2.at[mine], {"head": to})

    @pl.when((seq > 0) & (head < SINK_MOST))
    def _():
        remote(own.at[0], piece, ss1.at[0], rs1.at[0], {"seq": 0}).wait_recv()

    @pl.when(head < SINK_MOST)
    def _():
        for k in (2, 1, 3):
            piece_far(k).start()
        pieces[head] = piece[...]

    lax.fori_loop(0, N, mark, 0)
    score_all(SINK_MOST, own)

    for copy in first:
        copy.wait_recv()
    for k in range(N):
        for c in range(CAP):
            slots_out[k, c] = rows_in[jnp.minimum(marks[k * CAP + c], N - 1)]
    second = exchange(slots_out, slots_in, s2, r2, seq, "seq")
    slots_in[seq] = slots_out[seq]

    @pl.when((mine < SINK_MOST) & (head >= SINK_MOST))
    def _():
        remote(piece, pieces.at[mine], ss2.at[0], rs2.at[mine], {"head": mine}).wait_recv()

    @pl.when(mine < SINK_MOST)
    def _():
        for k in NEAR:
            piece_near(k).start()

    relay(1)
    score_all(SINK_MOST + 1, win.at[0])
    slot_of = places()

    for b in range(SINK_MOST):

        @pl.when(mine != b)
        def _():
            remote(piece, pieces.at[b], ss2.at[0], rs2.at[b], {"head": b}).wait_recv()

    spread = []
    for k in ORDER:
        to = lax.rem(seq + k, N)
        spread.append(remote(pieces, sink.at[seq], ss3.at[k], rs3.at[k], {"seq": to}))
        spread[-1].start()
    sink[seq] = pieces[...]

    for copy in second:
        copy.wait_recv()
    for k in range(N):
        far_out[k] = slots_in[slot_of[k] >> 1, slot_of[k] & 1]
    third = exchange(far_out, kept, s3, r3, head, "head")
    kept[head] = far_out[head]

    relay(2)
    score_all(SINK_MOST + 2, win.at[1])

    for copy in spread:
        copy.wait_recv()
    lax.fori_loop(0, KVH, score_sinks, 0, unroll=2)
    for copy in steps[2 * CHUNKS :]:
        copy.wait_recv()
    score_all(SINK_MOST + 3, win.at[2])
    for copy in third:
        copy.wait_recv()


    def kept_step(g, carry):
        score(g, SLOTS - 1, part(kept, g, 0), part(kept, g, 1), efar, dfar)
        combine(g)

        def put(side, x):
            tkept[pl.ds(4 * g, 4), side] = x.astype(low)

        grad(g, SLOTS - 1, efar, dfar, put)
        return carry

    lax.fori_loop(0, KVH, kept_step, 0, unroll=True)
    first_back = exchange(tkept, rows, t1, v1, head, "head")
    rows[head] = tkept[head]
    rows[N] = jnp.zeros(PIECE, low)

    lax.fori_loop(0, KVH, grad_sinks, 0, unroll=2)
    spread_back = exchange(tsink, sink_in, ts3, vs3, seq, "seq")
    sink_in[seq] = tsink[seq]

    def put_hop(at, side, x):
        hop_out[0, at, side] = x.astype(low)

    grad_all(SLOTS - 2, put_hop)
    hops = []

    def hop(w):
        for c in range(CHUNKS):
            at = pl.ds(c * (N // CHUNKS), N // CHUNKS)
            i = w * CHUNKS + c
            if w > 0:
                hops[i - CHUNKS].wait_recv()
                hop_out[w, at] = (near[WIN_MOST - 1 - w, at] + hop_in[w - 1, at].astype(wide)).astype(low)
            hops.append(remote(hop_out.at[w, at], hop_in.at[w, at], tw.at[i], vw.at[i], before))
            hops[i].start()

    hop(0)
    lax.fori_loop(0, N * CAP, fill, 0)

    def put_near(n):
        def put(at, side, x):
            near[n, at, side] = x

        return put

    grad_all(SINK_MOST + 2, put_near(2))

    for copy in first_back:
        copy.wait_recv()
    for k in range(N):
        for c in range(CAP):
            back_out[k, c] = rows[fills[k * CAP + c]]
    second_back = exchange(back_out, back_in, t2, v2, seq, "seq")
    back_in[seq] = back_out[seq]

    for copy in spread_back:
        copy.wait_recv()
    for b in range(SINK_MOST):
        term = sink_in[0, b].astype(wide)
        for k in range(1, N):
            term = term + sink_in[k, b].astype(wide)
        shares[b] = term.astype(low)

    def share_near(b):
        r = lax.rem(head + 4 - b, 4)
        to = lax.rem(jnp.where(r == 3, head + 1, head + N - r), N)
        return remote(shares.at[b], shares_in.at[r], ts2.at[b], vs2.at[r], {"head": to})

    for b in range(SINK_MOST):

        @pl.when(mine != b)
        def _():
            share_near(b).start()

    hop(1)
    grad_all(SINK_MOST + 1, put_near(1))

    def share_far():
        k = 3 + head // 4
        return remote(share, shares_far.at[k - 4], ts2.at[3], vs2.at[k], {"head": mine})

    @pl.when(mine < SINK_MOST)
    def _():
        term = shares[mine].astype(wide)
        for k in range(1, 4):
            remote(shares.at[0], shares_in.at[k], ts2.at[3], vs2.at[k], {"head": mine}).wait_recv()
            term = term + shares_in[k].astype(wide)
        share[...] = term

    @pl.when((mine < SINK_MOST) & (head >= SINK_MOST))
    def _():
        share_far().start()

    lax.fori_loop(0, N * CAP, link, 0)
    lax.fori_loop(0, N, last, 0)
    run[...] = jnp.zeros(run.shape, wide)

    for copy in second_back:
        copy.wait_recv()
    for k in range(N):
        for c in range(CAP):
            i = k * CAP + c
            run[i] = back_in[k, c].astype(wide) + run[links[i]]
    for k in range(N):
        sums[k] = run[lasts[k]].astype(low)
    third_back = exchange(sums, sums_in, t3, v3, head, "head")
    sums_in[head] = sums[head]

    hop(2)

    grad_all(SINK_MOST, put_near(0))

    for g in range(KVH):
        turned = lax.dot_general(kbuf[g], sbuf[g], TN, preferred_element_type=wide)
        m = g % 2
        dqbuf[:, GROUP * m : GROUP * (m + 1), :] = (turned.T * scale).reshape(BLK, GROUP, HD)
        if m == 1:
            dq[:, GROUP * (g - 1) : GROUP * (g + 1), :] = dqbuf[...].astype(low)

    def whole_send():
        return remote(whole_out, whole.at[seq], ts1.at[0], vs1.at[seq], {"seq": 0})

    @pl.when(head < SINK_MOST)
    def _():
        term = share[...]
        for k in range(4, 7):
            remote(share, shares_far.at[k - 4], ts2.at[3], vs2.at[k], {"head": mine}).wait_recv()
            term = term + shares_far[k - 4]
        whole_out[...] = term

    @pl.when((head < SINK_MOST) & (seq > 0))
    def _():
        whole_send().start()

    for copy in hops[2 * CHUNKS :]:
        copy.wait_recv()
    total[...] = near[0] + hop_in[2].astype(wide)
    for copy in third_back:
        copy.wait_recv()
    total[...] = total[...] + sums_in[...].astype(wide)

    @pl.when((head < SINK_MOST) & (seq == 0))
    def _():
        whole[0] = whole_out[...]
        for k in range(1, N):
            remote(whole_out, whole.at[k], ts1.at[0], vs1.at[k], {"seq": k}).wait_recv()
        total[...] = total[...] + whole[...]

    for side, ref in ((0, dk), (1, dv)):
        heads = [total[4 * g : 4 * (g + 1), side].reshape(BLK, HD) for g in range(KVH)]
        ref[...] = jnp.stack(heads, axis=1).astype(low)


    for copy in steps + first + second + third + spread:
        copy.wait_send()
    for copy in hops + first_back + second_back + third_back + spread_back:
        copy.wait_send()

    @pl.when((seq == 0) & (head < SINK_MOST))
    def _():
        for k in range(1, N):
            sink_send(k).wait_send()

    @pl.when(head < SINK_MOST)
    def _():
        for k in (2, 1, 3):
            piece_far(k).wait_send()

    @pl.when(mine < SINK_MOST)
    def _():
        for k in NEAR:
            piece_near(k).wait_send()

    for b in range(SINK_MOST):

        @pl.when(mine != b)
        def _():
            share_near(b).wait_send()

    @pl.when((mine < SINK_MOST) & (head >= SINK_MOST))
    def _():
        share_far().wait_send()

    @pl.when((head < SINK_MOST) & (seq > 0))
    def _():
        whole_send().wait_send()


def attend(kept_blocks, sink_blocks, window_blocks, q, g, keys, values):
    low, wide = jnp.bfloat16, jnp.float32
    vmem = pl.BlockSpec(memory_space=pltpu.VMEM)
    smem = pl.BlockSpec(memory_space=pltpu.SMEM)
    hbm = pl.BlockSpec(memory_space=pl.ANY)
    dma = pltpu.SemaphoreType.DMA

    def lows(*lead):
        return pltpu.VMEM(lead + PIECE, low)

    def wides(*lead):
        return pltpu.VMEM(lead + PIECE, wide)

    raw = pltpu.VMEM((BLK, KVH * GROUP, HD), low)
    flat = pltpu.VMEM((KVH, COLUMNS, HD), low)
    rows = pltpu.VMEM((KVH, SLOTS, COLUMNS), wide)
    return pl.pallas_call(
        kernel,
        out_shape=(
            jax.ShapeDtypeStruct((BLK, KVH * GROUP, HD), low),
            jax.ShapeDtypeStruct((BLK, KVH, HD), low),
            jax.ShapeDtypeStruct((BLK, KVH, HD), low),
        ),
        in_specs=[smem, smem, smem, hbm, hbm, vmem, vmem],
        out_specs=(vmem, vmem, vmem),
        scratch_shapes=[
            lows(N),
            lows(N), lows(N, CAP), lows(N, CAP), lows(N), lows(), lows(SINK_MOST),
            lows(N, SINK_MOST), lows(WIN_MOST - 1, N), lows(N),
            lows(N, SINK_MOST), lows(N), wides(WIN_MOST - 1, N), lows(N + 1), lows(N, CAP), lows(N, CAP),
            wides(N * CAP + 1), lows(N), lows(N),
            lows(N, SINK_MOST), lows(SINK_MOST), lows(4), wides(3), wides(), wides(), wides(N),
            lows(WIN_MOST - 1, N), lows(WIN_MOST - 1, N), wides(N),
            raw, raw, flat, flat,
            pltpu.VMEM((KVH, SLOTS * BLK, HD), low),
            pltpu.VMEM((KVH, SLOTS - 1, BLK, COLUMNS), wide),
            pltpu.VMEM((KVH, SLOTS - 1, BLK, COLUMNS), wide),
            pltpu.VMEM((KVH, SLOTS * BLK, COLUMNS), low),
            pltpu.VMEM((BLK, COLUMNS), wide),
            pltpu.VMEM((BLK, COLUMNS), wide),
            rows, rows, rows, rows,
            pltpu.VMEM((KVH, 1, COLUMNS), wide),
            pltpu.VMEM((BLK, 2 * GROUP, HD), wide),
            pltpu.SMEM((N * CAP,), jnp.int32), pltpu.SMEM((N * CAP,), jnp.int32),
            pltpu.SMEM((N * CAP,), jnp.int32), pltpu.SMEM((N,), jnp.int32),
            dma((2,)),
            dma((3 * CHUNKS,)), dma((3 * CHUNKS,)), dma((N,)), dma((N,)), dma((N,)), dma((N,)), dma((N,)), dma((N,)),
            dma((N,)), dma((1,)), dma((N,)), dma((N,)), dma((N,)), dma((N,)),
            dma((3 * CHUNKS,)), dma((3 * CHUNKS,)), dma((N,)), dma((N,)), dma((N,)), dma((N,)), dma((N,)), dma((N,)),
            dma((1,)), dma((N,)), dma((4,)), dma((8,)), dma((N,)), dma((N,)),
        ],
        compiler_params=pltpu.CompilerParams(
            collective_id=0, has_side_effects=True, vmem_limit_bytes=VMEM_LIMIT
        ),
        name="attend",
    )(kept_blocks, sink_blocks, window_blocks, q, g, keys, values)


def body(queries, keys, values, out_grad, kept_blocks, sink_blocks, window_blocks):
    lists = kept_blocks.reshape(KVH, N * N)
    return attend(lists, sink_blocks, window_blocks, queries, out_grad, keys, values)


def solution(mesh):
    tokens = P(("dp", "seq", "head"), None, None)
    return jax.shard_map(
        body,
        mesh=mesh,
        in_specs=(tokens, tokens, tokens, tokens, P(), P(), P()),
        out_specs=(tokens, tokens, tokens),
        check_vma=False,
    )
```
